768 devices in a mesh: context: 24 (over z, core), channel: 8 (over y), dp: 4 (over x).
Axes of the slice: x: 4, y: 8, z: 12, core: 2. Of those that a mesh axis runs over, the one named last changes fastest.
Arguments:
- features: bfloat16 [4, 12288, 3, 2048], P('dp', 'context', None, 'channel'), may hold values from -6 to 6
- doc_start: int32 [4, 24], P('dp'), may hold values 0 or 1
- short_taps: float32 [3, 3, 2048], P(None, None, 'channel'), may hold values from -3 to 3
- long_filter: bfloat16 [2048, 2048], P('channel', 'dp'), may hold values from -0.125 to 0.125
- w_out: bfloat16 [2048, 2048], P('channel'), may hold values from -0.125 to 0.125
Outputs:
- layer_out: bfloat16 [4, 12288, 2048], P('dp', ('context', 'channel'))
The draws below stay inside these ranges and needn't reach their ends.
Inputs may be any that keep to these rules, and one draw needn't show every extreme that they name: `doc_start`: block 0 of every sequence begins a document whatever its entry.
All inputs are finite; a program needn't handle non-finite values.
Results may differ from the reference program's by a relative error of at most 0.023.
Values may be sent and summed in bfloat16 or wider, within the bound.
A program may use at most 64 MiB of HBM per device.

```python
import jax
import jax.numpy as jnp
from jax import lax

L = 512
SEGS = 4
CHAN = 2048
DOUT = 2048
REPLICAS = 4
GROUPS = 24
TOKENS = 12288
N_CHANNEL = 8


def set_ends(drawn, rng, least, largest):
    dims = drawn.shape
    spot = [jax.random.randint(jax.random.fold_in(rng, axis), (), 0, dims[axis]) for axis in range(len(dims))]
    drawn = drawn.at[tuple(spot)].set(least)
    longest = dims.index(max(dims))
    spot[longest] = (spot[longest] + 1) % dims[longest]
    return drawn.at[tuple(spot)].set(largest)


def shard_levels(own_key, extent, pieces, low, largest):
    factor_of = 1.0
    for dim, parts in pieces:
        heights = jax.random.uniform(jax.random.fold_in(jax.random.fold_in(own_key, 6), dim), (parts,), jnp.float32, low / len(pieces), largest / len(pieces))
        factor_of = factor_of * jnp.repeat(jnp.exp(heights), extent[dim] // parts).reshape((-1,) + (1,) * (len(extent) - 1 - dim))
    return factor_of


def centred(key, extent, spread, limit, pieces=(), kind=jnp.bfloat16):
    gain = shard_levels(key, extent, pieces, -0.22, 0.18) if pieces else 1.0
    values = jax.random.normal(key, extent, jnp.float32) * spread * gain
    return jnp.minimum(jnp.maximum(values, -limit), limit).astype(kind)


def setup_inputs(seed: int = 0) -> dict:
    keys = jax.random.split(jax.random.key(seed), 6)
    features = centred(keys[0], (REPLICAS, TOKENS, 3, CHAN), 1.0, 6.0, ((0, 4), (1, 24), (3, 8)))
    doc_start = set_ends((jax.random.randint(keys[1], (REPLICAS, GROUPS), 0, 4) < 1).astype(jnp.int32), jax.random.fold_in(keys[1], 1), 0, 1)
    short_taps = centred(keys[2], (3, 3, CHAN), 0.6, 3.0, ((2, 8),), jnp.float32)
    long_filter = centred(keys[3], (CHAN, SEGS * L), (SEGS * L) ** -0.5, 0.125, ((0, 8), (1, 4)))
    w_out = centred(keys[4], (CHAN, DOUT), CHAN ** -0.5, 0.125, ((0, 8),))
    return dict(features=features, doc_start=doc_start, short_taps=short_taps, long_filter=long_filter, w_out=w_out)


def filter_spectra(long_filter):
    taps = long_filter.astype(jnp.float32).reshape(CHAN, SEGS, L)
    padded = jnp.concatenate([taps, jnp.zeros_like(taps)], 2)
    return jnp.transpose(jnp.fft.rfft(padded, axis=2), (1, 2, 0))


def one_replica(features, doc_start, short_taps, spectra, w_out):
    position = jnp.arange(GROUPS)
    begins = jnp.where(position == 0, 1, doc_start).astype(jnp.int32)
    documents = jnp.cumsum(begins).astype(jnp.int32)
    token_doc = jnp.repeat(documents, L)
    streams = features.astype(jnp.float32)
    smoothed = jnp.zeros(streams.shape, jnp.float32)
    for delay in range(3):
        moved = jnp.concatenate([jnp.zeros((delay,) + streams.shape[1:], jnp.float32), streams[:TOKENS - delay]], 0)
        moved_doc = jnp.concatenate([jnp.full((delay,), -1, jnp.int32), token_doc[:TOKENS - delay]], 0)
        same = (moved_doc == token_doc)[:, None, None]
        smoothed = smoothed + short_taps[delay][None] * jnp.where(same, moved, jnp.float32(0.0))
    product = (smoothed[:, 1] * smoothed[:, 2]).astype(jnp.bfloat16)
    blocks = product.astype(jnp.float32).reshape(GROUPS, L, CHAN)
    earlier = jnp.concatenate([jnp.zeros_like(blocks[:1]), blocks[:-1]], 0)
    earlier = jnp.where(begins[:, None, None] == 1, jnp.float32(0.0), earlier)
    windows = jnp.concatenate([earlier, blocks], 1)
    source = jnp.fft.rfft(windows, axis=1)
    total = jnp.zeros_like(source)
    for offset in range(SEGS):
        moved = jnp.concatenate([jnp.zeros_like(source[:offset]), source[:GROUPS - offset]], 0)
        moved_doc = jnp.concatenate([jnp.full((offset,), -1, jnp.int32), documents[:GROUPS - offset]], 0)
        same = (moved_doc == documents)[:, None, None]
        total = total + jnp.where(same, spectra[offset][None] * moved, jnp.zeros_like(moved))
    conv = jnp.fft.irfft(total, n=2 * L, axis=1)[:, L:, :].reshape(TOKENS, CHAN)
    gated = (smoothed[:, 0] * conv).astype(jnp.bfloat16)
    width = CHAN // N_CHANNEL
    summed = jnp.zeros((TOKENS, DOUT), jnp.float32)
    for block in range(N_CHANNEL):
        part = jnp.dot(gated[:, block * width:(block + 1) * width], w_out[block * width:(block + 1) * width], preferred_element_type=jnp.float32)
        summed = summed + lax.optimization_barrier(part.astype(jnp.bfloat16)).astype(jnp.float32)
    return summed.astype(jnp.bfloat16)


def reference(features, doc_start, short_taps, long_filter, w_out):
    spectra = filter_spectra(long_filter)

    def single(pair):
        return one_replica(pair[0], pair[1], short_taps, spectra, w_out)

    return lax.map(single, (features, doc_start))
```

```python
import functools

import jax
import jax.numpy as jnp
import numpy as np
from jax import lax
from jax.experimental import pallas as pl
from jax.experimental.pallas import tpu as pltpu
from jax.sharding import PartitionSpec as P

MESH = pl.DeviceIdType.MESH
F32 = jnp.float32
BF16 = jnp.bfloat16
HALF = 128


def tables(block_len):
    freq = np.concatenate([np.arange(0, block_len, 2), np.arange(1, block_len, 2)])
    angle = 2.0 * np.pi * ((2 * freq[:, None] + 1) * np.arange(block_len)[None, :] % (4 * block_len)) / (4 * block_len)
    sign = np.where(freq % 2 == 0, 1.0, -1.0)[:, None]
    forward = np.concatenate([np.cos(angle), -np.sin(angle)], 0)
    inverse = np.concatenate([-sign * np.sin(angle), -sign * np.cos(angle)], 0).T / block_len
    return forward.astype(jnp.bfloat16), inverse.astype(jnp.bfloat16)


def kernel(
    sizes, doc, taps, x, filt, w, fwd, inv, out,
    ext, fbuf, ibuf, wbuf, pbuf, rbuf, tbuf, fspec, gspec, spec, qbuf, acc, total, cown, csend, crecv, gated, sbuf, vbuf,
    load_sem, tail_sem, tap_send, tap_recv, halo_send, halo_recv, swap_send, swap_recv, ring_send, ring_recv,
):
    n_ctx, n_ch, n_dp, block_len, d_out = sizes
    chips = n_ctx // 2
    ctx = lax.axis_index("context")
    y = lax.axis_index("channel")
    xi = lax.axis_index("dp")
    z = ctx // 2
    c = ctx % 2
    piece = block_len // n_ch
    sub = d_out // 4
    steps = n_ch - 1

    def chip(distance):
        return lax.rem(z + distance + chips, chips)

    barrier = pltpu.get_barrier_semaphore()
    pl.semaphore_signal(barrier, inc=1, device_id={"context": 2 * z + 1 - c}, device_id_type=MESH)
    for distance in (-1, -2):
        for core in (0, 1):
            pl.semaphore_signal(barrier, inc=1, device_id={"context": 2 * chip(distance) + core}, device_id_type=MESH)
    for by in range(1, n_dp):
        pl.semaphore_signal(barrier, inc=1, device_id={"dp": lax.rem(xi + by, n_dp)}, device_id_type=MESH)
    for by in (1, n_ch - 1):
        pl.semaphore_signal(barrier, inc=1, device_id={"channel": lax.rem(y + by, n_ch)}, device_id_type=MESH)

    own_rows = pl.ds(pl.multiple_of(c * HALF, HALF), HALF)
    loads = [
        pltpu.make_async_copy(x, ext.at[:, pl.ds(16, block_len), :], load_sem.at[0]),
        pltpu.make_async_copy(filt.at[own_rows, :], tbuf.at[xi], load_sem.at[1]),
        pltpu.make_async_copy(fwd, fbuf, load_sem.at[2]),
        pltpu.make_async_copy(inv, ibuf, load_sem.at[3]),
        pltpu.make_async_copy(w, wbuf, load_sem.at[4]),
    ]
    for load in loads:
        load.start()
    pl.semaphore_wait(barrier, 4 + n_dp + 2)

    tail = pltpu.make_async_remote_copy(
        src_ref=x.at[:, pl.ds(block_len - 16, 16), :], dst_ref=ext.at[:, pl.ds(0, 16), :],
        send_sem=tail_sem.at[0], recv_sem=tail_sem.at[1],
        device_id={"context": lax.rem(ctx + 1, n_ctx)}, device_id_type=MESH)
    tail.start()

    def tap_copy(by):
        return pltpu.make_async_remote_copy(
            src_ref=filt.at[own_rows, :], dst_ref=tbuf.at[xi],
            send_sem=tap_send.at[by - 1], recv_sem=tap_recv.at[by - 1],
            device_id={"dp": lax.rem(xi + by, n_dp)}, device_id_type=MESH)

    for by in range(1, n_dp):
        tap_copy(by).start()

    def goes_on(block):
        at = jnp.maximum(block, 0)
        return jnp.where((block > 0) & (doc[0, at] != 1), 1.0, 0.0).astype(F32)

    own_goes_on = goes_on(ctx)
    keep_b = goes_on(2 * z + 1)
    keep1 = goes_on(2 * z)
    keep2 = keep1 * goes_on(2 * z - 1)
    keep3 = keep2 * goes_on(2 * z - 2)
    keep4 = keep3 * goes_on(2 * z - 3)

    chunk = min(128, block_len)

    def smooth(stream, start):
        rows = ext[stream, pl.ds(start, chunk + 16), :].astype(F32)
        got = (
            taps[0, pl.ds(stream, 1), :] * rows
            + taps[1, pl.ds(stream, 1), :] * pltpu.roll(rows, 1, 0)
            + taps[2, pl.ds(stream, 1), :] * pltpu.roll(rows, 2, 0)
        )
        return got[16:]

    def make_product(start):
        product = (smooth(1, start) * smooth(2, start)).astype(BF16)
        pbuf[0, pl.ds(start, chunk), :] = product[:, :HALF]
        pbuf[1, pl.ds(start, chunk), :] = product[:, HALF:]

    loads[0].wait()
    for start in range(chunk, block_len, chunk):
        make_product(start)
    tail.wait_recv()
    for stream in range(3):
        ext[stream, pl.ds(0, 16), :] = (ext[stream, pl.ds(0, 16), :].astype(F32) * own_goes_on).astype(BF16)
    make_product(0)

    def halo_copy(distance, half):
        return pltpu.make_async_remote_copy(
            src_ref=pbuf.at[half], dst_ref=rbuf.at[distance, c],
            send_sem=halo_send.at[distance, half], recv_sem=halo_recv.at[distance, c],
            device_id={"context": 2 * chip(distance) + half}, device_id_type=MESH)

    def halo_arrived(distance, core):
        pltpu.make_async_remote_copy(
            src_ref=pbuf.at[0], dst_ref=rbuf.at[distance, core],
            send_sem=halo_send.at[distance, 0], recv_sem=halo_recv.at[distance, core],
            device_id={"context": ctx}, device_id_type=MESH).wait_recv()

    halo_copy(0, 1 - c).start()
    for distance in (1, 2):
        for half in (0, 1):
            halo_copy(distance, half).start()
    rbuf[0, c] = pbuf[c]

    for start in range(0, block_len, chunk):
        smoothed = smooth(0, start)
        qbuf[0, pl.ds(start, chunk), :] = smoothed[:, :HALF]
        qbuf[1, pl.ds(start, chunk), :] = smoothed[:, HALF:]

    loads[1].wait()
    loads[2].wait()
    for by in range(1, n_dp):
        tap_copy(by).wait_recv()
    taps_all = tbuf[...].reshape(n_dp * HALF, block_len)
    tile = block_len // 2

    def filter_rows(i, carry):
        rows = pl.ds(pl.multiple_of(i * tile, tile), tile)
        fspec[rows, :] = lax.dot_general(
            fbuf[rows, :], tbuf[...].reshape(n_dp * HALF, block_len), (((1,), (1,)), ((), ())), preferred_element_type=F32)
        return carry

    lax.fori_loop(0, 4, filter_rows, 0)

    step_rows = min(64, block_len // 2)
    tiles = block_len // step_rows

    def places(i):
        at = pl.multiple_of(i * step_rows, step_rows)
        return pl.ds(at, step_rows), pl.ds(block_len + at, step_rows)

    def combine(i, carry):
        re, im = places(i)
        sign = (1 - 2 * (i // (tiles // 2))).astype(F32)
        for d in range(n_dp + 1):
            real = imag = None
            if d > 0:
                lanes = pl.ds((d - 1) * HALF, HALF)
                real, imag = fspec[re, lanes], fspec[im, lanes]
            if d < n_dp:
                lanes = pl.ds(d * HALF, HALF)
                more_real, more_imag = sign * fspec[im, lanes], -sign * fspec[re, lanes]
                real = more_real if real is None else real + more_real
                imag = more_imag if imag is None else imag + more_imag
            gspec[d, re, :] = real
            gspec[d, im, :] = imag
        return carry

    lax.fori_loop(0, tiles, combine, 0)

    def transform(distance, keep_lo, keep_hi):
        lo, hi = rbuf[distance, 0], rbuf[distance, 1]
        if keep_lo is not None:
            lo = (lo.astype(F32) * keep_lo).astype(BF16)
            hi = (hi.astype(F32) * keep_hi).astype(BF16)
        rbuf[distance, 0] = lo
        rbuf[distance, 1] = hi

        def rows_of(i, carry):
            rows = pl.ds(pl.multiple_of(i * tile, tile), tile)
            both = jnp.concatenate([rbuf[distance, 0], rbuf[distance, 1]], 1)
            spec[distance, rows, :] = jnp.dot(fbuf[rows, :], both, preferred_element_type=F32)
            return carry

        lax.fori_loop(0, 4, rows_of, 0)

    def term(d, distance, core, re, im):
        lanes = pl.ds(core * HALF, HALF)
        a, b = gspec[d, re, :], gspec[d, im, :]
        u, v = spec[distance, re, lanes], spec[distance, im, lanes]
        return a * u - b * v, a * v + b * u

    def terms(which, re, im):
        got = [term(d, distance, core, re, im) for d, distance, core in which]
        return sum(g[0] for g in got[1:]) + got[0][0], sum(g[1] for g in got[1:]) + got[0][1]

    halo_arrived(0, 1 - c)
    transform(0, None, None)
    for core in (0, 1):
        halo_arrived(1, core)
    transform(1, keep2, keep1)

    def early(i, carry):
        re, im = places(i)
        real, imag = terms([(0, 0, 0), (1, 1, 1), (2, 1, 0)], re, im)
        acc[0, re, :] = real
        acc[0, im, :] = imag
        real, imag = terms([(1, 0, 0), (2, 1, 1), (3, 1, 0)], re, im)
        acc[1, re, :] = real
        acc[1, im, :] = imag
        return carry

    lax.fori_loop(0, tiles, early, 0)
    for core in (0, 1):
        halo_arrived(2, core)
    transform(2, keep4, keep3)

    def late(i, carry):
        re, im = places(i)
        real, imag = terms([(3, 2, 1), (4, 2, 0)], re, im)
        total[re, pl.ds(0, HALF)] = (acc[0, re, :] + real).astype(BF16)
        total[im, pl.ds(0, HALF)] = (acc[0, im, :] + imag).astype(BF16)
        real, imag = terms([(4, 2, 1)], re, im)
        own_real, own_imag = terms([(0, 0, 1)], re, im)
        total[re, pl.ds(HALF, HALF)] = (own_real + keep_b * (acc[1, re, :] + real)).astype(BF16)
        total[im, pl.ds(HALF, HALF)] = (own_imag + keep_b * (acc[1, im, :] + imag)).astype(BF16)
        return carry

    lax.fori_loop(0, tiles, late, 0)

    loads[3].wait()

    def swap_copy(i):
        rows = pl.ds(i * chunk, chunk)
        return pltpu.make_async_remote_copy(
            src_ref=csend.at[rows, :], dst_ref=crecv.at[rows, :],
            send_sem=swap_send.at[i], recv_sem=swap_recv.at[i],
            device_id={"context": 2 * z + 1 - c}, device_id_type=MESH)

    own_first = (1 - c).astype(F32)
    own_second = c.astype(F32)
    for i in range(block_len // chunk):
        rows = pl.ds(i * chunk, chunk)
        conv = jnp.dot(ibuf[rows, :], total[...], preferred_element_type=F32)
        cown[0, rows, :] = conv[:, :HALF]
        cown[1, rows, :] = conv[:, HALF:]
        csend[rows, :] = cown[1 - c, rows, :].astype(BF16)
        swap_copy(i).start()
        gated[c, rows, :] = (qbuf[c, rows, :] * cown[c, rows, :]).astype(BF16)
    for i in range(block_len // chunk):
        rows = pl.ds(i * chunk, chunk)
        swap_copy(i).wait_recv()
        gated[1 - c, rows, :] = (qbuf[1 - c, rows, :] * crecv[rows, :].astype(F32)).astype(BF16)

    loads[4].wait()

    def ring_copy(s, q):
        to = lax.rem(y + (1 if q < 2 else n_ch - 1), n_ch)
        return pltpu.make_async_remote_copy(
            src_ref=sbuf.at[s, q], dst_ref=vbuf.at[s, q],
            send_sem=ring_send.at[s, q], recv_sem=ring_recv.at[s, q],
            device_id={"channel": to}, device_id_type=MESH)

    def project(j, q):
        rows = pl.ds(pl.multiple_of(j * piece, piece), piece)
        lhs = jnp.concatenate([gated[0, rows, :], gated[1, rows, :]], 1)
        return jnp.dot(lhs, wbuf[:, q * sub:(q + 1) * sub], preferred_element_type=F32)

    def ring_step(s, first):
        up = lax.rem(y - 1 - s + 2 * n_ch, n_ch)
        down = lax.rem(y + 1 + s, n_ch)
        for q in (0, 2, 1, 3):
            part = project(up if q < 2 else down, q)
            if not first:
                ring_copy(s - 1, q).wait_recv()
                part = part + vbuf[s - 1, q].astype(F32)
            sbuf[s, q] = part.astype(BF16)
            ring_copy(s, q).start()

    ring_step(0, True)

    def ring_body(s, carry):
        ring_step(s, False)
        return carry

    lax.fori_loop(1, steps, ring_body, 0)
    for q in (0, 2, 1, 3):
        part = project(y, q)
        ring_copy(steps - 1, q).wait_recv()
        out[:, q * sub:(q + 1) * sub] = (part + vbuf[steps - 1, q].astype(F32)).astype(BF16)

    tail.wait_send()
    for by in range(1, n_dp):
        tap_copy(by).wait_send()
    halo_copy(0, 1 - c).wait_send()
    for distance in (1, 2):
        for half in (0, 1):
            halo_copy(distance, half).wait_send()
    for i in range(block_len // chunk):
        swap_copy(i).wait_send()

    def sent(s, carry):
        for q in range(4):
            ring_copy(s, q).wait_send()
        return carry

    lax.fori_loop(0, steps, sent, 0)


def per_device(mesh_shape, features, doc_start, short_taps, long_filter, w_out):
    block_len, channels, d_out = features.shape[1], features.shape[3], w_out.shape[1]
    n_ctx, n_ch, n_dp = mesh_shape["context"], mesh_shape["channel"], mesh_shape["dp"]
    streams = jnp.transpose(features[0], (1, 0, 2))
    forward, inverse = tables(block_len)
    piece, sub, steps = block_len // n_ch, d_out // 4, n_ch - 1
    width = 2 * block_len
    swaps = block_len // min(128, block_len)
    anywhere = pl.BlockSpec(memory_space=pl.ANY)
    vmem = pl.BlockSpec(memory_space=pltpu.VMEM)
    dma = pltpu.SemaphoreType.DMA
    result = pl.pallas_call(
        functools.partial(kernel, (n_ctx, n_ch, n_dp, block_len, d_out)),
        out_shape=jax.ShapeDtypeStruct((piece, d_out), BF16),
        in_specs=[pl.BlockSpec(memory_space=pltpu.SMEM), vmem] + [anywhere] * 5,
        out_specs=vmem,
        scratch_shapes=[
            pltpu.VMEM((3, 16 + block_len, channels), BF16),
            pltpu.VMEM((width, block_len), BF16),
            pltpu.VMEM((block_len, width), BF16),
            pltpu.VMEM((channels, d_out), BF16),
            pltpu.VMEM((2, block_len, HALF), BF16),
            pltpu.VMEM((3, 2, block_len, HALF), BF16),
            pltpu.VMEM((n_dp, HALF, block_len), BF16),
            pltpu.VMEM((width, n_dp * HALF), F32),
            pltpu.VMEM((n_dp + 1, width, HALF), F32),
            pltpu.VMEM((3, width, 2 * HALF), F32),
            pltpu.VMEM((2, block_len, HALF), F32),
            pltpu.VMEM((2, width, HALF), F32),
            pltpu.VMEM((width, 2 * HALF), BF16),
            pltpu.VMEM((2, block_len, HALF), F32),
            pltpu.VMEM((block_len, HALF), BF16),
            pltpu.VMEM((block_len, HALF), BF16),
            pltpu.VMEM((2, block_len, HALF), BF16),
            pltpu.VMEM((steps, 4, piece, sub), BF16),
            pltpu.VMEM((steps, 4, piece, sub), BF16),
            dma((5,)), dma((2,)), dma((n_dp - 1,)), dma((n_dp - 1,)), dma((3, 2)), dma((3, 2)),
            dma((swaps,)), dma((swaps,)), dma((steps, 4)), dma((steps, 4)),
        ],
        compiler_params=pltpu.CompilerParams(
            collective_id=0, has_side_effects=True, vmem_limit_bytes=48 * 1024 * 1024),
    )(doc_start, short_taps, streams, long_filter, w_out, forward, inverse)
    return result[None]


def solution(mesh):
    return jax.shard_map(
        functools.partial(per_device, dict(mesh.shape)),
        mesh=mesh,
        in_specs=(
            P("dp", "context", None, "channel"),
            P("dp", None),
            P(None, None, "channel"),
            P("channel", "dp"),
            P("channel", None),
        ),
        out_specs=P("dp", ("context", "channel"), None),
        check_vma=False,
    )
```

```python
import functools

import jax
import jax.numpy as jnp
import numpy as np
from jax import lax
from jax.experimental import pallas as pl
from jax.experimental.pallas import tpu as pltpu
from jax.sharding import PartitionSpec as P

MESH = pl.DeviceIdType.MESH
F32 = jnp.float32
BF16 = jnp.bfloat16
SUBS = 8
HALF = 128


def tables(block_len):
    freq = np.concatenate([np.arange(0, block_len, 2), np.arange(1, block_len, 2)])
    angle = 2.0 * np.pi * ((2 * freq[:, None] + 1) * np.arange(block_len)[None, :] % (4 * block_len)) / (4 * block_len)
    sign = np.where(freq % 2 == 0, 1.0, -1.0)[:, None]
    forward = np.concatenate([np.cos(angle), -np.sin(angle)], 0)
    inverse = np.concatenate([-sign * np.sin(angle), -sign * np.cos(angle)], 0).T / block_len
    return forward.astype(jnp.bfloat16), inverse.astype(jnp.bfloat16)


def kernel(
    sizes, doc_in, taps_in, x, filt, w, fwd, inv, out,
    doc, taps, ext, fbuf, ibuf, wbuf, pbuf, rbuf, tbuf, fspec, gspec, spec, qbuf, acc, total, cown, csend, crecv, gated, sbuf, vbuf,
    load_sem, tail_sem, tap_send, tap_recv, halo_send, halo_recv, swap_send, swap_recv, ring_send, ring_recv,
):
    n_ctx, n_ch, n_dp, block_len, d_out = sizes
    chips = n_ctx // 2
    ctx = lax.axis_index("context")
    y = lax.axis_index("channel")
    xi = lax.axis_index("dp")
    z = ctx // 2
    c = ctx % 2
    piece = block_len // n_ch
    sub = d_out // SUBS
    order = [i // 2 + (i % 2) * (SUBS // 2) for i in range(SUBS)]
    steps = n_ch - 1

    def chip(distance):
        return lax.rem(z + distance + chips, chips)

    barrier = pltpu.get_barrier_semaphore()
    pl.semaphore_signal(barrier, inc=1, device_id={"context": 2 * z + 1 - c}, device_id_type=MESH)
    for distance in (1, 2):
        @pl.when(z >= distance)
        def _():
            for core in (0, 1):
                pl.semaphore_signal(barrier, inc=1, device_id={"context": 2 * chip(-distance) + core}, device_id_type=MESH)
    for by in range(1, n_dp):
        pl.semaphore_signal(barrier, inc=1, device_id={"dp": lax.rem(xi + by, n_dp)}, device_id_type=MESH)
    for by in (1, n_ch - 1):
        pl.semaphore_signal(barrier, inc=1, device_id={"channel": lax.rem(y + by, n_ch)}, device_id_type=MESH)

    own_rows = pl.ds(pl.multiple_of(c * HALF, HALF), HALF)
    loads = [
        pltpu.make_async_copy(x, ext.at[:, pl.ds(16, block_len), :], load_sem.at[0]),
        pltpu.make_async_copy(filt.at[own_rows, :], tbuf.at[xi], load_sem.at[1]),
        pltpu.make_async_copy(fwd, fbuf, load_sem.at[2]),
        pltpu.make_async_copy(inv, ibuf, load_sem.at[3]),
        pltpu.make_async_copy(w, wbuf, load_sem.at[4]),
        pltpu.make_async_copy(doc_in, doc, load_sem.at[5]),
        pltpu.make_async_copy(taps_in, taps, load_sem.at[6]),
    ]
    for load in loads:
        load.start()
    def tap_copy(by):
        return pltpu.make_async_remote_copy(
            src_ref=filt.at[own_rows, :], dst_ref=tbuf.at[xi],
            send_sem=tap_send.at[by - 1], recv_sem=tap_recv.at[by - 1],
            device_id={"dp": lax.rem(xi + by, n_dp)}, device_id_type=MESH)

    loads[5].wait()
    loads[6].wait()

    def goes_on(block):
        at = jnp.maximum(block, 0)
        return jnp.where((block > 0) & (doc[0, at] != 1), 1.0, 0.0).astype(F32)

    own_goes_on = goes_on(ctx)
    keep_b = goes_on(2 * z + 1)
    keep1 = goes_on(2 * z)
    keep2 = keep1 * goes_on(2 * z - 1)
    keep3 = keep2 * goes_on(2 * z - 2)
    keep4 = keep3 * goes_on(2 * z - 3)

    chunk = min(128, block_len)

    def smooth(stream, start, count):
        rows = ext[stream, pl.ds(start, count + 16), :].astype(F32)
        got = (
            taps[0, pl.ds(stream, 1), :] * rows
            + taps[1, pl.ds(stream, 1), :] * pltpu.roll(rows, 1, 0)
            + taps[2, pl.ds(stream, 1), :] * pltpu.roll(rows, 2, 0)
        )
        return got[16:]

    def make_product(start, count):
        product = (smooth(1, start, count) * smooth(2, start, count)).astype(BF16)
        pbuf[0, pl.ds(start, count), :] = product[:, :HALF]
        pbuf[1, pl.ds(start, count), :] = product[:, HALF:]

    def make_gate(start, count):
        smoothed = smooth(0, start, count)
        qbuf[0, pl.ds(start, count), :] = smoothed[:, :HALF]
        qbuf[1, pl.ds(start, count), :] = smoothed[:, HALF:]

    parts = (pl.ds(16, block_len - 16), pl.ds(0, 16))

    def halo_copy(distance, half, part):
        return pltpu.make_async_remote_copy(
            src_ref=pbuf.at[half, parts[part], :], dst_ref=rbuf.at[distance, c, parts[part], :],
            send_sem=halo_send.at[distance, half, part], recv_sem=halo_recv.at[distance, c, part],
            device_id={"context": 2 * chip(distance) + half}, device_id_type=MESH)

    def halo_arrived(distance, core):
        for part in (0, 1):
            pltpu.make_async_remote_copy(
                src_ref=pbuf.at[0, parts[part], :], dst_ref=rbuf.at[distance, core, parts[part], :],
                send_sem=halo_send.at[distance, 0, part], recv_sem=halo_recv.at[distance, core, part],
                device_id={"context": ctx}, device_id_type=MESH).wait_recv()

    def each_halo(act, parts_of):
        for distance in (2, 1):
            @pl.when(z + distance < chips)
            def _():
                for part in parts_of:
                    for half in (0, 1):
                        act(halo_copy(distance, half, part))
        for part in parts_of:
            act(halo_copy(0, 1 - c, part))

    loads[0].wait()
    for start in range(0, block_len, chunk):
        first = max(start, 16)
        make_product(first, start + chunk - first)

    ahead = jnp.where(z + 1 < chips, 2, 0) + jnp.where(z + 2 < chips, 2, 0)
    pl.semaphore_wait(barrier, 1 + ahead + (n_dp - 1) + 2)

    tail = pltpu.make_async_remote_copy(
        src_ref=x.at[:, pl.ds(block_len - 16, 16), :], dst_ref=ext.at[:, pl.ds(0, 16), :],
        send_sem=tail_sem.at[0], recv_sem=tail_sem.at[1],
        device_id={"context": lax.rem(ctx + 1, n_ctx)}, device_id_type=MESH)

    @pl.when(ctx + 1 < n_ctx)
    def _():
        tail.start()

    each_halo(lambda copy: copy.start(), (0,))
    for by in range(1, n_dp):
        tap_copy(by).start()

    for start in range(0, block_len, chunk):
        first = max(start, 16)
        make_gate(first, start + chunk - first)
    for distance in (1, 2):
        @pl.when(z < distance)
        def _():
            rbuf[distance] = jnp.zeros(rbuf.shape[1:], BF16)

    @pl.when(ctx > 0)
    def _():
        tail.wait_recv()

    @pl.when(ctx == 0)
    def _():
        ext[:, pl.ds(0, 16), :] = jnp.zeros((3, 16, ext.shape[2]), BF16)

    for stream in range(3):
        ext[stream, pl.ds(0, 16), :] = (ext[stream, pl.ds(0, 16), :].astype(F32) * own_goes_on).astype(BF16)
    make_product(0, 16)
    each_halo(lambda copy: copy.start(), (1,))
    make_gate(0, 16)
    rbuf[0, c] = pbuf[c]

    loads[1].wait()
    loads[2].wait()
    for by in range(1, n_dp):
        tap_copy(by).wait_recv()
    tile = block_len // 2

    def filter_rows(i, carry):
        rows = pl.ds(pl.multiple_of(i * tile, tile), tile)
        fspec[rows, :] = lax.dot_general(
            fbuf[rows, :], tbuf[...].reshape(n_dp * HALF, block_len), (((1,), (1,)), ((), ())), preferred_element_type=F32)
        return carry

    lax.fori_loop(0, 4, filter_rows, 0)

    step_rows = min(64, block_len // 2)
    tiles = block_len // step_rows

    def places(i):
        at = pl.multiple_of(i * step_rows, step_rows)
        return pl.ds(at, step_rows), pl.ds(block_len + at, step_rows)

    def combine(i, carry):
        re, im = places(i)
        sign = (1 - 2 * (i // (tiles // 2))).astype(F32)
        for d in range(n_dp + 1):
            real = imag = None
            if d > 0:
                lanes = pl.ds((d - 1) * HALF, HALF)
                real, imag = fspec[re, lanes], fspec[im, lanes]
            if d < n_dp:
                lanes = pl.ds(d * HALF, HALF)
                more_real, more_imag = sign * fspec[im, lanes], -sign * fspec[re, lanes]
                real = more_real if real is None else real + more_real
                imag = more_imag if imag is None else imag + more_imag
            gspec[d, re, :] = real
            gspec[d, im, :] = imag
        return carry

    lax.fori_loop(0, tiles, combine, 0)

    def transform(distance, keep_lo, keep_hi):
        lo, hi = rbuf[distance, 0], rbuf[distance, 1]
        if keep_lo is not None:
            lo = (lo.astype(F32) * keep_lo).astype(BF16)
            hi = (hi.astype(F32) * keep_hi).astype(BF16)
        rbuf[distance, 0] = lo
        rbuf[distance, 1] = hi

        def rows_of(i, carry):
            rows = pl.ds(pl.multiple_of(i * tile, tile), tile)
            both = jnp.concatenate([rbuf[distance, 0], rbuf[distance, 1]], 1)
            spec[distance, rows, :] = jnp.dot(fbuf[rows, :], both, preferred_element_type=F32)
            return carry

        lax.fori_loop(0, 4, rows_of, 0)

    def term(d, distance, core, re, im):
        lanes = pl.ds(core * HALF, HALF)
        a, b = gspec[d, re, :], gspec[d, im, :]
        u, v = spec[distance, re, lanes], spec[distance, im, lanes]
        return a * u - b * v, a * v + b * u

    def terms(which, re, im):
        got = [term(d, distance, core, re, im) for d, distance, core in which]
        return sum(g[0] for g in got[1:]) + got[0][0], sum(g[1] for g in got[1:]) + got[0][1]

    halo_arrived(0, 1 - c)
    transform(0, None, None)

    @pl.when(z >= 1)
    def _():
        for core in (0, 1):
            halo_arrived(1, core)

    transform(1, keep2, keep1)

    def early(i, carry):
        re, im = places(i)
        real, imag = terms([(0, 0, 0), (1, 1, 1), (2, 1, 0)], re, im)
        acc[0, re, :] = real
        acc[0, im, :] = imag
        real, imag = terms([(1, 0, 0), (2, 1, 1), (3, 1, 0)], re, im)
        acc[1, re, :] = real
        acc[1, im, :] = imag
        return carry

    lax.fori_loop(0, tiles, early, 0)

    @pl.when(z >= 2)
    def _():
        for core in (0, 1):
            halo_arrived(2, core)

    transform(2, keep4, keep3)

    def late(i, carry):
        re, im = places(i)
        real, imag = terms([(3, 2, 1), (4, 2, 0)], re, im)
        total[re, pl.ds(0, HALF)] = (acc[0, re, :] + real).astype(BF16)
        total[im, pl.ds(0, HALF)] = (acc[0, im, :] + imag).astype(BF16)
        real, imag = terms([(4, 2, 1)], re, im)
        own_real, own_imag = terms([(0, 0, 1)], re, im)
        total[re, pl.ds(HALF, HALF)] = (own_real + keep_b * (acc[1, re, :] + real)).astype(BF16)
        total[im, pl.ds(HALF, HALF)] = (own_imag + keep_b * (acc[1, im, :] + imag)).astype(BF16)
        return carry

    lax.fori_loop(0, tiles, late, 0)

    loads[3].wait()

    def swap_copy(i):
        rows = pl.ds(i * chunk, chunk)
        return pltpu.make_async_remote_copy(
            src_ref=csend.at[rows, :], dst_ref=crecv.at[rows, :],
            send_sem=swap_send.at[i], recv_sem=swap_recv.at[i],
            device_id={"context": 2 * z + 1 - c}, device_id_type=MESH)

    own_first = (1 - c).astype(F32)
    own_second = c.astype(F32)
    for i in range(block_len // chunk):
        rows = pl.ds(i * chunk, chunk)
        conv = jnp.dot(ibuf[rows, :], total[...], preferred_element_type=F32)
        cown[0, rows, :] = conv[:, :HALF]
        cown[1, rows, :] = conv[:, HALF:]
        csend[rows, :] = cown[1 - c, rows, :].astype(BF16)
        swap_copy(i).start()
        gated[c, rows, :] = (qbuf[c, rows, :] * cown[c, rows, :]).astype(BF16)
    for i in range(block_len // chunk):
        rows = pl.ds(i * chunk, chunk)
        swap_copy(i).wait_recv()
        gated[1 - c, rows, :] = (qbuf[1 - c, rows, :] * crecv[rows, :].astype(F32)).astype(BF16)

    loads[4].wait()

    def ring_copy(s, q):
        to = lax.rem(y + (1 if q < SUBS // 2 else n_ch - 1), n_ch)
        return pltpu.make_async_remote_copy(
            src_ref=sbuf.at[s, q], dst_ref=vbuf.at[s, q],
            send_sem=ring_send.at[s, q], recv_sem=ring_recv.at[s, q],
            device_id={"channel": to}, device_id_type=MESH)

    def project(j, q):
        rows = pl.ds(pl.multiple_of(j * piece, piece), piece)
        lhs = jnp.concatenate([gated[0, rows, :], gated[1, rows, :]], 1)
        return jnp.dot(lhs, wbuf[:, q * sub:(q + 1) * sub], preferred_element_type=F32)

    def ring_step(s, first):
        up = lax.rem(y - 1 - s + 2 * n_ch, n_ch)
        down = lax.rem(y + 1 + s, n_ch)
        for q in order:
            part = project(up if q < SUBS // 2 else down, q)
            if not first:
                ring_copy(s - 1, q).wait_recv()
                part = part + vbuf[s - 1, q].astype(F32)
            sbuf[s, q] = part.astype(BF16)
            ring_copy(s, q).start()

    ring_step(0, True)

    def ring_body(s, carry):
        ring_step(s, False)
        return carry

    lax.fori_loop(1, steps, ring_body, 0)
    for q in order:
        part = project(y, q)
        ring_copy(steps - 1, q).wait_recv()
        out[:, q * sub:(q + 1) * sub] = (part + vbuf[steps - 1, q].astype(F32)).astype(BF16)

    @pl.when(ctx + 1 < n_ctx)
    def _():
        tail.wait_send()

    for by in range(1, n_dp):
        tap_copy(by).wait_send()
    each_halo(lambda copy: copy.wait_send(), (0, 1))
    for i in range(block_len // chunk):
        swap_copy(i).wait_send()

    def sent(s, carry):
        for q in range(SUBS):
            ring_copy(s, q).wait_send()
        return carry

    lax.fori_loop(0, steps, sent, 0)


def per_device(mesh_shape, features, doc_start, short_taps, long_filter, w_out):
    block_len, channels, d_out = features.shape[1], features.shape[3], w_out.shape[1]
    n_ctx, n_ch, n_dp = mesh_shape["context"], mesh_shape["channel"], mesh_shape["dp"]
    streams = jnp.transpose(features[0], (1, 0, 2))
    forward, inverse = tables(block_len)
    piece, sub, steps = block_len // n_ch, d_out // SUBS, n_ch - 1
    width = 2 * block_len
    swaps = block_len // min(128, block_len)
    anywhere = pl.BlockSpec(memory_space=pltpu.HBM)
    vmem = pl.BlockSpec(memory_space=pltpu.VMEM)
    dma = pltpu.SemaphoreType.DMA
    result = pl.pallas_call(
        functools.partial(kernel, (n_ctx, n_ch, n_dp, block_len, d_out)),
        out_shape=jax.ShapeDtypeStruct((piece, d_out), BF16),
        in_specs=[anywhere] * 7,
        out_specs=vmem,
        scratch_shapes=[
            pltpu.SMEM(doc_start.shape, jnp.int32),
            pltpu.VMEM(short_taps.shape, F32),
            pltpu.VMEM((3, 16 + block_len, channels), BF16),
            pltpu.VMEM((width, block_len), BF16),
            pltpu.VMEM((block_len, width), BF16),
            pltpu.VMEM((channels, d_out), BF16),
            pltpu.VMEM((2, block_len, HALF), BF16),
            pltpu.VMEM((3, 2, block_len, HALF), BF16),
            pltpu.VMEM((n_dp, HALF, block_len), BF16),
            pltpu.VMEM((width, n_dp * HALF), F32),
            pltpu.VMEM((n_dp + 1, width, HALF), F32),
            pltpu.VMEM((3, width, 2 * HALF), F32),
            pltpu.VMEM((2, block_len, HALF), F32),
            pltpu.VMEM((2, width, HALF), F32),
            pltpu.VMEM((width, 2 * HALF), BF16),
            pltpu.VMEM((2, block_len, HALF), F32),
            pltpu.VMEM((block_len, HALF), BF16),
            pltpu.VMEM((block_len, HALF), BF16),
            pltpu.VMEM((2, block_len, HALF), BF16),
            pltpu.VMEM((steps, SUBS, piece, sub), BF16),
            pltpu.VMEM((steps, SUBS, piece, sub), BF16),
            dma((7,)), dma((2,)), dma((n_dp - 1,)), dma((n_dp - 1,)), dma((3, 2, 2)), dma((3, 2, 2)),
            dma((swaps,)), dma((swaps,)), dma((steps, SUBS)), dma((steps, SUBS)),
        ],
        compiler_params=pltpu.CompilerParams(
            collective_id=0, has_side_effects=True, vmem_limit_bytes=60 * 1024 * 1024),
    )(doc_start, short_taps, streams, long_filter, w_out, forward, inverse)
    return result[None]


def solution(mesh):
    return jax.shard_map(
        functools.partial(per_device, dict(mesh.shape)),
        mesh=mesh,
        in_specs=(
            P("dp", "context", None, "channel"),
            P("dp", None),
            P(None, None, "channel"),
            P("channel", "dp"),
            P("channel", None),
        ),
        out_specs=P("dp", ("context", "channel"), None),
        check_vma=False,
    )
```

```python
import functools

import jax
import jax.numpy as jnp
import numpy as np
from jax import lax
from jax.experimental import pallas as pl
from jax.experimental.pallas import tpu as pltpu
from jax.sharding import PartitionSpec as P

MESH = pl.DeviceIdType.MESH
F32 = jnp.float32
BF16 = jnp.bfloat16
HALF = 128


def tables(block_len):
    freq = np.concatenate([np.arange(0, block_len, 2), np.arange(1, block_len, 2)])
    angle = 2.0 * np.pi * ((2 * freq[:, None] + 1) * np.arange(block_len)[None, :] % (4 * block_len)) / (4 * block_len)
    sign = np.where(freq % 2 == 0, 1.0, -1.0)[:, None]
    forward = np.concatenate([np.cos(angle), -np.sin(angle)], 0)
    inverse = np.concatenate([-sign * np.sin(angle), -sign * np.cos(angle)], 0).T / block_len
    return forward.astype(jnp.bfloat16), inverse.astype(jnp.bfloat16)


def kernel(
    sizes, doc_in, taps_in, x, filt, w, fwd, inv, out,
    doc, taps, ext, fbuf, ibuf, wall, pbuf, rbuf, tbuf, fspec, gspec, spec, qbuf, qsend, acc, total,
    gown, gall, gpair, osum, psend, precv, rsend, rrecv,
    load_sem, tail_sem, tap_send, tap_recv, halo_send, halo_recv, q_sem, w_send, w_recv,
    g_send, g_recv, f_send, f_recv, p_send, p_recv, r_sem,
):
    n_ctx, n_ch, n_dp, block_len, d_out = sizes
    chips = n_ctx // 2
    ctx = lax.axis_index("context")
    y = lax.axis_index("channel")
    xi = lax.axis_index("dp")
    z = ctx // 2
    c = ctx % 2
    piece = block_len // n_ch
    columns = d_out // 2
    sibling = {"context": 2 * z + 1 - c}
    side = xi % 2
    partner = {"dp": xi + 1 - 2 * side}

    def chip(distance):
        return lax.rem(z + distance + chips, chips)

    barrier = pltpu.get_barrier_semaphore()
    pl.semaphore_signal(barrier, inc=1, device_id=sibling, device_id_type=MESH)
    for distance in (1, 2):
        @pl.when(z >= distance)
        def _():
            for core in (0, 1):
                pl.semaphore_signal(barrier, inc=1, device_id={"context": 2 * chip(-distance) + core}, device_id_type=MESH)
    for by in range(1, n_dp):
        pl.semaphore_signal(barrier, inc=1, device_id={"dp": lax.rem(xi + by, n_dp)}, device_id_type=MESH)
    for by in range(1, n_ch):
        pl.semaphore_signal(barrier, inc=1, device_id={"channel": lax.rem(y + by, n_ch)}, device_id_type=MESH)

    own_rows = pl.ds(pl.multiple_of(c * HALF, HALF), HALF)
    loads = [
        pltpu.make_async_copy(x, ext.at[:, pl.ds(16, block_len), :], load_sem.at[0]),
        pltpu.make_async_copy(filt.at[own_rows, :], tbuf.at[xi], load_sem.at[1]),
        pltpu.make_async_copy(fwd, fbuf, load_sem.at[2]),
        pltpu.make_async_copy(inv, ibuf, load_sem.at[3]),
        pltpu.make_async_copy(
            w.at[own_rows, pl.ds(pl.multiple_of(side * columns, 128), columns)], wall.at[y], load_sem.at[4]),
        pltpu.make_async_copy(doc_in, doc, load_sem.at[5]),
        pltpu.make_async_copy(taps_in, taps, load_sem.at[6]),
    ]
    for load in loads:
        load.start()
    def tap_copy(by):
        return pltpu.make_async_remote_copy(
            src_ref=filt.at[own_rows, :], dst_ref=tbuf.at[xi],
            send_sem=tap_send.at[by - 1], recv_sem=tap_recv.at[by - 1],
            device_id={"dp": lax.rem(xi + by, n_dp)}, device_id_type=MESH)

    loads[5].wait()
    loads[6].wait()

    def goes_on(block):
        at = jnp.maximum(block, 0)
        return jnp.where((block > 0) & (doc[0, at] != 1), 1.0, 0.0).astype(F32)

    own_goes_on = goes_on(ctx)
    keep_b = goes_on(2 * z + 1)
    keep1 = goes_on(2 * z)
    keep2 = keep1 * goes_on(2 * z - 1)
    keep3 = keep2 * goes_on(2 * z - 2)
    keep4 = keep3 * goes_on(2 * z - 3)

    chunk = min(128, block_len)

    def smooth(stream, start, count):
        rows = ext[stream, pl.ds(start, count + 16), :].astype(F32)
        got = (
            taps[0, pl.ds(stream, 1), :] * rows
            + taps[1, pl.ds(stream, 1), :] * pltpu.roll(rows, 1, 0)
            + taps[2, pl.ds(stream, 1), :] * pltpu.roll(rows, 2, 0)
        )
        return got[16:]

    def make_product(start, count):
        product = (smooth(1, start, count) * smooth(2, start, count)).astype(BF16)
        pbuf[0, pl.ds(start, count), :] = product[:, :HALF]
        pbuf[1, pl.ds(start, count), :] = product[:, HALF:]

    def make_gate(start, count):
        smoothed = smooth(0, start, count).astype(BF16)
        qsend[0, pl.ds(start, count), :] = smoothed[:, :HALF]
        qsend[1, pl.ds(start, count), :] = smoothed[:, HALF:]

    parts = (pl.ds(16, block_len - 16), pl.ds(0, 16))

    def halo_copy(distance, half, part):
        return pltpu.make_async_remote_copy(
            src_ref=pbuf.at[half, parts[part], :], dst_ref=rbuf.at[distance, c, parts[part], :],
            send_sem=halo_send.at[distance, half, part], recv_sem=halo_recv.at[distance, c, part],
            device_id={"context": 2 * chip(distance) + half}, device_id_type=MESH)

    def halo_arrived(distance, core):
        for part in (0, 1):
            pltpu.make_async_remote_copy(
                src_ref=pbuf.at[0, parts[part], :], dst_ref=rbuf.at[distance, core, parts[part], :],
                send_sem=halo_send.at[distance, 0, part], recv_sem=halo_recv.at[distance, core, part],
                device_id={"context": ctx}, device_id_type=MESH).wait_recv()

    def each_halo(act, parts_of):
        for distance in (2, 1):
            @pl.when(z + distance < chips)
            def _():
                for part in parts_of:
                    for half in (0, 1):
                        act(halo_copy(distance, half, part))
        for part in parts_of:
            act(halo_copy(0, 1 - c, part))

    loads[0].wait()
    for start in range(0, block_len, chunk):
        first = max(start, 16)
        make_product(first, start + chunk - first)

    ahead = jnp.where(z + 1 < chips, 2, 0) + jnp.where(z + 2 < chips, 2, 0)
    pl.semaphore_wait(barrier, 1 + ahead + (n_dp - 1) + (n_ch - 1))

    tail = pltpu.make_async_remote_copy(
        src_ref=x.at[:, pl.ds(block_len - 16, 16), :], dst_ref=ext.at[:, pl.ds(0, 16), :],
        send_sem=tail_sem.at[0], recv_sem=tail_sem.at[1],
        device_id={"context": lax.rem(ctx + 1, n_ctx)}, device_id_type=MESH)

    @pl.when(ctx + 1 < n_ctx)
    def _():
        tail.start()

    each_halo(lambda copy: copy.start(), (0,))

    w_steps = n_ch // 2

    def w_copy(way, step):
        by = (1, n_ch - 1)[way]
        source = lax.rem(y + (n_ch - by) * (step - 1), n_ch)
        lanes = pl.ds(0, columns) if step < w_steps else pl.ds(way * (columns // 2), columns // 2)
        return pltpu.make_async_remote_copy(
            src_ref=wall.at[source, :, lanes], dst_ref=wall.at[source, :, lanes],
            send_sem=w_send.at[way, step - 1], recv_sem=w_recv.at[way, step - 1],
            device_id={"channel": lax.rem(y + by, n_ch)}, device_id_type=MESH)

    def w_arrived(way, step):
        by = (1, n_ch - 1)[way]
        source = lax.rem(y + (n_ch - by) * step, n_ch)
        lanes = pl.ds(0, columns) if step < w_steps else pl.ds(way * (columns // 2), columns // 2)
        pltpu.make_async_remote_copy(
            src_ref=wall.at[source, :, lanes], dst_ref=wall.at[source, :, lanes],
            send_sem=w_send.at[way, step - 1], recv_sem=w_recv.at[way, step - 1],
            device_id={"channel": lax.rem(y + by, n_ch)}, device_id_type=MESH).wait_recv()

    def pass_on(step):
        if step < w_steps:
            for way in (0, 1):
                w_arrived(way, step)
                w_copy(way, step + 1).start()

    loads[4].wait()
    for way in (0, 1):
        w_copy(way, 1).start()
    for by in range(1, n_dp):
        tap_copy(by).start()

    for start in range(0, block_len, chunk):
        first = max(start, 16)
        make_gate(first, start + chunk - first)
    for distance in (1, 2):
        @pl.when(z < distance)
        def _():
            rbuf[distance] = jnp.zeros(rbuf.shape[1:], BF16)

    @pl.when(ctx > 0)
    def _():
        tail.wait_recv()

    @pl.when(ctx == 0)
    def _():
        ext[:, pl.ds(0, 16), :] = jnp.zeros((3, 16, ext.shape[2]), BF16)

    for stream in range(3):
        ext[stream, pl.ds(0, 16), :] = (ext[stream, pl.ds(0, 16), :].astype(F32) * own_goes_on).astype(BF16)
    make_product(0, 16)
    each_halo(lambda copy: copy.start(), (1,))
    make_gate(0, 16)
    q_copy = pltpu.make_async_remote_copy(
        src_ref=qsend.at[1 - c], dst_ref=qbuf.at[c], send_sem=q_sem.at[0], recv_sem=q_sem.at[1],
        device_id=sibling, device_id_type=MESH)
    q_copy.start()
    qbuf[c] = qsend[c]
    rbuf[0, c] = pbuf[c]

    loads[1].wait()
    loads[2].wait()
    for by in range(1, n_dp):
        tap_copy(by).wait_recv()
    tile = block_len // 2

    def filter_rows(i, carry):
        rows = pl.ds(pl.multiple_of(i * tile, tile), tile)
        fspec[rows, :] = lax.dot_general(
            fbuf[rows, :], tbuf[...].reshape(n_dp * HALF, block_len), (((1,), (1,)), ((), ())), preferred_element_type=F32)
        return carry

    lax.fori_loop(0, 4, filter_rows, 0)

    step_rows = min(64, block_len // 2)
    tiles = block_len // step_rows

    def places(i):
        at = pl.multiple_of(i * step_rows, step_rows)
        return pl.ds(at, step_rows), pl.ds(block_len + at, step_rows)

    def combine(i, carry):
        re, im = places(i)
        sign = (1 - 2 * (i // (tiles // 2))).astype(F32)
        for d in range(n_dp + 1):
            real = imag = None
            if d > 0:
                lanes = pl.ds((d - 1) * HALF, HALF)
                real, imag = fspec[re, lanes], fspec[im, lanes]
            if d < n_dp:
                lanes = pl.ds(d * HALF, HALF)
                more_real, more_imag = sign * fspec[im, lanes], -sign * fspec[re, lanes]
                real = more_real if real is None else real + more_real
                imag = more_imag if imag is None else imag + more_imag
            gspec[d, re, :] = real
            gspec[d, im, :] = imag
        return carry

    lax.fori_loop(0, tiles, combine, 0)
    pass_on(1)

    def transform(distance, keep_lo, keep_hi):
        lo, hi = rbuf[distance, 0], rbuf[distance, 1]
        if keep_lo is not None:
            lo = (lo.astype(F32) * keep_lo).astype(BF16)
            hi = (hi.astype(F32) * keep_hi).astype(BF16)
        rbuf[distance, 0] = lo
        rbuf[distance, 1] = hi

        def rows_of(i, carry):
            rows = pl.ds(pl.multiple_of(i * tile, tile), tile)
            both = jnp.concatenate([rbuf[distance, 0], rbuf[distance, 1]], 1)
            spec[distance, rows, :] = jnp.dot(fbuf[rows, :], both, preferred_element_type=F32)
            return carry

        lax.fori_loop(0, 4, rows_of, 0)

    def term(d, distance, core, re, im):
        lanes = pl.ds(core * HALF, HALF)
        a, b = gspec[d, re, :], gspec[d, im, :]
        u, v = spec[distance, re, lanes], spec[distance, im, lanes]
        return a * u - b * v, a * v + b * u

    def terms(which, re, im):
        got = [term(d, distance, core, re, im) for d, distance, core in which]
        return sum(g[0] for g in got[1:]) + got[0][0], sum(g[1] for g in got[1:]) + got[0][1]

    halo_arrived(0, 1 - c)
    transform(0, None, None)

    @pl.when(z >= 1)
    def _():
        for core in (0, 1):
            halo_arrived(1, core)

    transform(1, keep2, keep1)

    def early(i, carry):
        re, im = places(i)
        real, imag = terms([(0, 0, 0), (1, 1, 1), (2, 1, 0)], re, im)
        acc[0, re, :] = real
        acc[0, im, :] = imag
        real, imag = terms([(1, 0, 0), (2, 1, 1), (3, 1, 0)], re, im)
        acc[1, re, :] = real
        acc[1, im, :] = imag
        return carry

    lax.fori_loop(0, tiles, early, 0)
    pass_on(2)

    @pl.when(z >= 2)
    def _():
        for core in (0, 1):
            halo_arrived(2, core)

    transform(2, keep4, keep3)

    def late(i, carry):
        re, im = places(i)
        real, imag = terms([(3, 2, 1), (4, 2, 0)], re, im)
        total[re, pl.ds(0, HALF)] = (acc[0, re, :] + real).astype(BF16)
        total[im, pl.ds(0, HALF)] = (acc[0, im, :] + imag).astype(BF16)
        real, imag = terms([(4, 2, 1)], re, im)
        own_real, own_imag = terms([(0, 0, 1)], re, im)
        total[re, pl.ds(HALF, HALF)] = (own_real + keep_b * (acc[1, re, :] + real)).astype(BF16)
        total[im, pl.ds(HALF, HALF)] = (own_imag + keep_b * (acc[1, im, :] + imag)).astype(BF16)
        return carry

    lax.fori_loop(0, tiles, late, 0)

    loads[3].wait()
    pltpu.make_async_remote_copy(
        src_ref=qsend.at[1 - c], dst_ref=qbuf.at[1 - c], send_sem=q_sem.at[0], recv_sem=q_sem.at[1],
        device_id=sibling, device_id_type=MESH).wait_recv()
    pairs = n_ch // 2
    own_pair = y // 2
    other = y + 1 - 2 * (y % 2)

    def g_copy(to):
        return pltpu.make_async_remote_copy(
            src_ref=gown.at[to], dst_ref=gall.at[y], send_sem=g_send.at[to], recv_sem=g_recv.at[y],
            device_id={"channel": to}, device_id_type=MESH)

    def g_arrived(source):
        pltpu.make_async_remote_copy(
            src_ref=gown.at[source], dst_ref=gall.at[source], send_sem=g_send.at[source], recv_sem=g_recv.at[source],
            device_id={"channel": other}, device_id_type=MESH).wait_recv()

    def f_copy(source):
        return pltpu.make_async_remote_copy(
            src_ref=gall.at[source], dst_ref=gpair.at[source], send_sem=f_send.at[source], recv_sem=f_recv.at[source],
            device_id=partner, device_id_type=MESH)

    for k in range(pairs):
        pair = lax.rem(own_pair + k, pairs)
        rows = pl.ds(pl.multiple_of(pair * 2 * piece, 2 * piece), 2 * piece)
        conv = jnp.dot(ibuf[rows, :], total[...], preferred_element_type=F32)
        for block in (0, 1):
            got = (qbuf[block, rows, :].astype(F32) * conv[:, block * HALF:(block + 1) * HALF]).astype(BF16)
            for i in (0, 1):
                gown[2 * pair + i, pl.ds(block * piece, piece), :] = got[i * piece:(i + 1) * piece]
        if k == 0:
            g_copy(other).start()
            gall[y] = gown[y]
            f_copy(y).start()
        else:
            for i in (0, 1):
                g_copy(2 * pair + i).start()
    pass_on(3)

    for k in range(pairs):
        pair = lax.rem(own_pair - k + pairs, pairs)
        for source in (other,) if k == 0 else (2 * pair, 2 * pair + 1):
            g_arrived(source)
            f_copy(source).start()
    for way in (0, 1):
        w_arrived(way, w_steps)

    mine = 2 * piece
    for k in range(pairs):
        pair = lax.rem(own_pair - k + pairs, pairs)
        weights = jnp.concatenate([wall[2 * pair], wall[2 * pair + 1]], 0)
        own = jnp.concatenate([gall[2 * pair], gall[2 * pair + 1]], 1)
        for i in (0, 1):
            f_copy(2 * pair + i).wait_recv()
        theirs = jnp.concatenate([gpair[2 * pair], gpair[2 * pair + 1]], 1)
        part = jnp.dot(jnp.concatenate([own, theirs], 0), weights, preferred_element_type=F32)
        if k == 0:
            osum[...] = part
        else:
            osum[...] += part

    def p_copy(i):
        return pltpu.make_async_remote_copy(
            src_ref=psend.at[i], dst_ref=precv.at[i], send_sem=p_send.at[i], recv_sem=p_recv.at[i],
            device_id=sibling, device_id_type=MESH)

    def rows_of_block(whose, block):
        return pl.ds(pl.multiple_of(whose * mine + block * piece, piece), piece)

    for whose in (1, 0):
        psend[whose] = osum[rows_of_block(whose, 1 - c), :].astype(BF16)
        p_copy(whose).start()
    back = pltpu.make_async_remote_copy(
        src_ref=rsend, dst_ref=rrecv, send_sem=r_sem.at[0], recv_sem=r_sem.at[1],
        device_id=partner, device_id_type=MESH)
    p_copy(1).wait_recv()
    rsend[...] = (osum[rows_of_block(1, c), :] + precv[1].astype(F32)).astype(BF16)
    back.start()
    p_copy(0).wait_recv()
    out[:, pl.ds(pl.multiple_of(side * columns, 128), columns)] = (
        osum[rows_of_block(0, c), :] + precv[0].astype(F32)).astype(BF16)
    back.wait_recv()
    out[:, pl.ds(pl.multiple_of((1 - side) * columns, 128), columns)] = rrecv[...]

    back.wait_send()
    q_copy.wait_send()
    for whose in (1, 0):
        p_copy(whose).wait_send()
    for step in range(1, w_steps + 1):
        for way in (0, 1):
            w_copy(way, step).wait_send()
    f_copy(y).wait_send()
    for by in range(1, n_ch):
        g_copy(lax.rem(y + by, n_ch)).wait_send()
        f_copy(lax.rem(y + by, n_ch)).wait_send()
    @pl.when(ctx + 1 < n_ctx)
    def _():
        tail.wait_send()

    for by in range(1, n_dp):
        tap_copy(by).wait_send()
    each_halo(lambda copy: copy.wait_send(), (0, 1))


def per_device(mesh_shape, features, doc_start, short_taps, long_filter, w_out):
    block_len, channels, d_out = features.shape[1], features.shape[3], w_out.shape[1]
    n_ctx, n_ch, n_dp = mesh_shape["context"], mesh_shape["channel"], mesh_shape["dp"]
    streams = jnp.transpose(features[0], (1, 0, 2))
    forward, inverse = tables(block_len)
    piece, columns = block_len // n_ch, d_out // 2
    width = 2 * block_len
    anywhere = pl.BlockSpec(memory_space=pltpu.HBM)
    vmem = pl.BlockSpec(memory_space=pltpu.VMEM)
    dma = pltpu.SemaphoreType.DMA
    result = pl.pallas_call(
        functools.partial(kernel, (n_ctx, n_ch, n_dp, block_len, d_out)),
        out_shape=jax.ShapeDtypeStruct((piece, d_out), BF16),
        in_specs=[anywhere] * 7,
        out_specs=vmem,
        scratch_shapes=[
            pltpu.SMEM(doc_start.shape, jnp.int32),
            pltpu.VMEM(short_taps.shape, F32),
            pltpu.VMEM((3, 16 + block_len, channels), BF16),
            pltpu.VMEM((width, block_len), BF16),
            pltpu.VMEM((block_len, width), BF16),
            pltpu.VMEM((n_ch, HALF, columns), BF16),
            pltpu.VMEM((2, block_len, HALF), BF16),
            pltpu.VMEM((3, 2, block_len, HALF), BF16),
            pltpu.VMEM((n_dp, HALF, block_len), BF16),
            pltpu.VMEM((width, n_dp * HALF), F32),
            pltpu.VMEM((n_dp + 1, width, HALF), F32),
            pltpu.VMEM((3, width, 2 * HALF), F32),
            pltpu.VMEM((2, block_len, HALF), BF16),
            pltpu.VMEM((2, block_len, HALF), BF16),
            pltpu.VMEM((2, width, HALF), F32),
            pltpu.VMEM((width, 2 * HALF), BF16),
            pltpu.VMEM((n_ch, 2 * piece, HALF), BF16),
            pltpu.VMEM((n_ch, 2 * piece, HALF), BF16),
            pltpu.VMEM((n_ch, 2 * piece, HALF), BF16),
            pltpu.VMEM((4 * piece, columns), F32),
            pltpu.VMEM((2, piece, columns), BF16),
            pltpu.VMEM((2, piece, columns), BF16),
            pltpu.VMEM((piece, columns), BF16),
            pltpu.VMEM((piece, columns), BF16),
            dma((7,)), dma((2,)), dma((n_dp - 1,)), dma((n_dp - 1,)), dma((3, 2, 2)), dma((3, 2, 2)), dma((2,)),
            dma((2, n_ch // 2)), dma((2, n_ch // 2)), dma((n_ch,)), dma((n_ch,)), dma((n_ch,)), dma((n_ch,)),
            dma((2,)), dma((2,)), dma((2,)),
        ],
        compiler_params=pltpu.CompilerParams(
            collective_id=0, has_side_effects=True, vmem_limit_bytes=60 * 1024 * 1024),
    )(doc_start, short_taps, streams, long_filter, w_out, forward, inverse)
    return result[None]


def solution(mesh):
    return jax.shard_map(
        functools.partial(per_device, dict(mesh.shape)),
        mesh=mesh,
        in_specs=(
            P("dp", "context", None, "channel"),
            P("dp", None),
            P(None, None, "channel"),
            P("channel", "dp"),
            P("channel", None),
        ),
        out_specs=P("dp", ("context", "channel"), None),
        check_vma=False,
    )
```

```python
import functools

import jax
import jax.numpy as jnp
import numpy as np
from jax import lax
from jax.experimental import pallas as pl
from jax.experimental.pallas import tpu as pltpu
from jax.sharding import PartitionSpec as P

MESH = pl.DeviceIdType.MESH
F32 = jnp.float32
BF16 = jnp.bfloat16
HALF = 128


def tables(block_len):
    freq = np.concatenate([np.arange(0, block_len, 2), np.arange(1, block_len, 2)])
    angle = 2.0 * np.pi * ((2 * freq[:, None] + 1) * np.arange(block_len)[None, :] % (4 * block_len)) / (4 * block_len)
    sign = np.where(freq % 2 == 0, 1.0, -1.0)[:, None]
    forward = np.concatenate([np.cos(angle), -np.sin(angle)], 0)
    inverse = np.concatenate([-sign * np.sin(angle), -sign * np.cos(angle)], 0).T / block_len
    return forward.astype(jnp.bfloat16), inverse.astype(jnp.bfloat16)


def kernel(
    sizes, doc_in, taps_in, x, filt, w, fwd, inv, out,
    doc, taps, ext, fbuf, ibuf, wall, pbuf, rbuf, tbuf, both, fspec, gspec, spec, qbuf, qsend, acc, total,
    gown, gall, gpair, osum, psend, precv, rsend, rrecv,
    load_sem, tail_sem, tap_send, tap_recv, halo_send, halo_recv, q_sem, w_send, w_recv, m_send, m_recv,
    g_send, g_recv, f_send, f_recv, p_send, p_recv, r_send, r_recv,
):
    n_ctx, n_ch, n_dp, block_len, d_out = sizes
    chips = n_ctx // 2
    ctx = lax.axis_index("context")
    y = lax.axis_index("channel")
    xi = lax.axis_index("dp")
    z = ctx // 2
    c = ctx % 2
    piece = block_len // n_ch
    columns = d_out // 2
    sibling = {"context": 2 * z + 1 - c}
    odd = xi % 2
    side = ((xi + 1) // 2) % 2
    partner = {"dp": xi + 1 - 2 * odd}
    mate = {"dp": lax.rem(xi + 2 * odd - 1 + n_dp, n_dp)}

    def chip(distance):
        return lax.rem(z + distance + chips, chips)

    barrier = pltpu.get_barrier_semaphore()
    pl.semaphore_signal(barrier, inc=1, device_id=sibling, device_id_type=MESH)

    @pl.when(z >= 1)
    def _():
        for core in (0, 1):
            pl.semaphore_signal(barrier, inc=1, device_id={"context": 2 * chip(-1) + core}, device_id_type=MESH)

    for by in range(1, n_dp):
        pl.semaphore_signal(barrier, inc=1, device_id={"dp": lax.rem(xi + by, n_dp)}, device_id_type=MESH)
    for by in range(1, n_ch):
        pl.semaphore_signal(barrier, inc=1, device_id={"channel": lax.rem(y + by, n_ch)}, device_id_type=MESH)

    own_rows = pl.ds(pl.multiple_of(c * HALF, HALF), HALF)
    loads = [
        pltpu.make_async_copy(x, ext.at[:, pl.ds(16, block_len), :], load_sem.at[0]),
        pltpu.make_async_copy(filt.at[own_rows, :], tbuf.at[xi], load_sem.at[1]),
        pltpu.make_async_copy(fwd, fbuf, load_sem.at[2]),
        pltpu.make_async_copy(inv, ibuf, load_sem.at[3]),
        pltpu.make_async_copy(
            w.at[own_rows, pl.ds(pl.multiple_of(side * columns, 128), columns)], wall.at[y], load_sem.at[4]),
        pltpu.make_async_copy(doc_in, doc, load_sem.at[5]),
        pltpu.make_async_copy(taps_in, taps, load_sem.at[6]),
    ]
    for load in loads:
        load.start()
    def tap_copy(by):
        return pltpu.make_async_remote_copy(
            src_ref=filt.at[own_rows, :], dst_ref=tbuf.at[xi],
            send_sem=tap_send.at[by - 1], recv_sem=tap_recv.at[by - 1],
            device_id={"dp": lax.rem(xi + by, n_dp)}, device_id_type=MESH)

    loads[5].wait()
    loads[6].wait()

    def goes_on(block):
        at = jnp.maximum(block, 0)
        return jnp.where((block > 0) & (doc[0, at] != 1), 1.0, 0.0).astype(F32)

    own_goes_on = goes_on(ctx)
    keep_b = goes_on(2 * z + 1)
    keep1 = goes_on(2 * z)
    keep2 = keep1 * goes_on(2 * z - 1)
    keep3 = keep2 * goes_on(2 * z - 2)
    keep4 = keep3 * goes_on(2 * z - 3)

    chunk = min(128, block_len)

    def smooth(stream, start, count):
        rows = ext[stream, pl.ds(start, count + 16), :].astype(F32)
        got = (
            taps[0, pl.ds(stream, 1), :] * rows
            + taps[1, pl.ds(stream, 1), :] * pltpu.roll(rows, 1, 0)
            + taps[2, pl.ds(stream, 1), :] * pltpu.roll(rows, 2, 0)
        )
        return got[16:]

    def make_product(start, count):
        product = (smooth(1, start, count) * smooth(2, start, count)).astype(BF16)
        pbuf[0, pl.ds(start, count), :] = product[:, :HALF]
        pbuf[1, pl.ds(start, count), :] = product[:, HALF:]

    def make_gate(start, count):
        smoothed = smooth(0, start, count).astype(BF16)
        qsend[0, pl.ds(start, count), :] = smoothed[:, :HALF]
        qsend[1, pl.ds(start, count), :] = smoothed[:, HALF:]

    middle = block_len // 2
    parts = (pl.ds(16, middle - 16), pl.ds(middle, middle), pl.ds(0, 16))

    def halo_copy(distance, half, part):
        return pltpu.make_async_remote_copy(
            src_ref=pbuf.at[half, parts[part], :], dst_ref=rbuf.at[distance, c, parts[part], :],
            send_sem=halo_send.at[distance, half, part], recv_sem=halo_recv.at[distance, c, part],
            device_id={"context": 2 * chip(distance) + half}, device_id_type=MESH)

    def forward_copy(core, part):
        return pltpu.make_async_remote_copy(
            src_ref=rbuf.at[1, core, parts[part], :], dst_ref=rbuf.at[2, core, parts[part], :],
            send_sem=halo_send.at[2, core, part], recv_sem=halo_recv.at[2, core, part],
            device_id={"context": 2 * chip(1) + c}, device_id_type=MESH)

    def halo_arrived(distance, core, part):
        pltpu.make_async_remote_copy(
            src_ref=pbuf.at[0, parts[part], :], dst_ref=rbuf.at[distance, core, parts[part], :],
            send_sem=halo_send.at[distance, 0, part], recv_sem=halo_recv.at[distance, core, part],
            device_id=sibling, device_id_type=MESH).wait_recv()

    def each_halo(act, parts_of):
        @pl.when(z + 1 < chips)
        def _():
            for part in parts_of:
                for half in (0, 1):
                    act(halo_copy(1, half, part))

        for part in parts_of:
            act(halo_copy(0, 1 - c, part))

    def take_in(parts_of):
        @pl.when(z >= 1)
        def _():
            for part in parts_of:
                for core in (0, 1):
                    halo_arrived(1, core, part)

        @pl.when((z >= 1) & (z + 1 < chips))
        def _():
            for part in parts_of:
                for core in (0, 1):
                    forward_copy(core, part).start()

    def make_products(lo, hi):
        for start in range(lo, hi, chunk):
            first = max(start, 16)
            make_product(first, start + chunk - first)

    loads[0].wait()
    make_products(0, 0 * chunk)
    ahead = jnp.where(z + 1 < chips, 2, 0)
    pl.semaphore_wait(barrier, 1 + ahead + (n_dp - 1) + (n_ch - 1))

    tail = pltpu.make_async_remote_copy(
        src_ref=x.at[:, pl.ds(block_len - 16, 16), :], dst_ref=ext.at[:, pl.ds(0, 16), :],
        send_sem=tail_sem.at[0], recv_sem=tail_sem.at[1],
        device_id={"context": lax.rem(ctx + 1, n_ctx)}, device_id_type=MESH)

    @pl.when(ctx + 1 < n_ctx)
    def _():
        tail.start()


    w_steps = n_ch // 2

    quarter = columns // 4

    def w_link(way, step, arriving):
        by = (1, n_ch - 1)[way]
        source = lax.rem(y + (n_ch - by) * (step if arriving else step - 1), n_ch)
        start, count = odd * quarter, 3 * quarter
        if step == w_steps:
            count = count // 2
            start = start + way * count
        lanes = pl.ds(pl.multiple_of(start, 128), count)
        return source, pltpu.make_async_remote_copy(
            src_ref=wall.at[source, :, lanes], dst_ref=wall.at[source, :, lanes],
            send_sem=w_send.at[way, step - 1], recv_sem=w_recv.at[way, step - 1],
            device_id={"channel": lax.rem(y + by, n_ch)}, device_id_type=MESH)

    def m_copy(source, arriving):
        lanes = pl.ds(pl.multiple_of(((1 - odd) if arriving else odd) * 3 * quarter, 128), quarter)
        return pltpu.make_async_remote_copy(
            src_ref=wall.at[source, :, lanes], dst_ref=wall.at[source, :, lanes],
            send_sem=m_send.at[source], recv_sem=m_recv.at[source], device_id=mate, device_id_type=MESH)

    def pass_on(step):
        if step < w_steps:
            for way in (0, 1):
                source, arrival = w_link(way, step, True)
                arrival.wait_recv()
                w_link(way, step + 1, False)[1].start()
                m_copy(source, False).start()

    loads[4].wait()
    for way in (0, 1):
        w_link(way, 1, False)[1].start()
    for by in range(1, n_dp):
        tap_copy(by).start()

    make_products(0 * chunk, block_len)
    each_halo(lambda copy: copy.start(), (0, 1))

    for start in range(0, block_len, chunk):
        first = max(start, 16)
        make_gate(first, start + chunk - first)
    for distance in (1, 2):
        @pl.when(z < distance)
        def _():
            rbuf[distance] = jnp.zeros(rbuf.shape[1:], BF16)

    @pl.when(ctx > 0)
    def _():
        tail.wait_recv()

    @pl.when(ctx == 0)
    def _():
        ext[:, pl.ds(0, 16), :] = jnp.zeros((3, 16, ext.shape[2]), BF16)

    for stream in range(3):
        ext[stream, pl.ds(0, 16), :] = (ext[stream, pl.ds(0, 16), :].astype(F32) * own_goes_on).astype(BF16)
    make_product(0, 16)
    each_halo(lambda copy: copy.start(), (2,))
    make_gate(0, 16)
    q_copy = pltpu.make_async_remote_copy(
        src_ref=qsend.at[1 - c], dst_ref=qbuf.at[c], send_sem=q_sem.at[0], recv_sem=q_sem.at[1],
        device_id=sibling, device_id_type=MESH)
    q_copy.start()
    qbuf[c] = qsend[c]
    rbuf[0, c] = pbuf[c]

    pass_on(1)

    loads[1].wait()
    loads[2].wait()
    for by in range(1, n_dp):
        tap_copy(by).wait_recv()
    tile = block_len // 2

    def filter_rows(i, carry):
        rows = pl.ds(pl.multiple_of(i * tile, tile), tile)
        fspec[rows, :] = lax.dot_general(
            fbuf[rows, :], tbuf[...].reshape(n_dp * HALF, block_len), (((1,), (1,)), ((), ())), preferred_element_type=F32)
        return carry

    take_in((0,))
    lax.fori_loop(0, 4, filter_rows, 0)
    take_in((1, 2))

    step_rows = min(64, block_len // 2)
    tiles = block_len // step_rows

    def places(i):
        at = pl.multiple_of(i * step_rows, step_rows)
        return pl.ds(at, step_rows), pl.ds(block_len + at, step_rows)

    def combine(i, carry):
        re, im = places(i)
        sign = (1 - 2 * (i // (tiles // 2))).astype(F32)
        for d in range(n_dp + 1):
            real = imag = None
            if d > 0:
                lanes = pl.ds((d - 1) * HALF, HALF)
                real, imag = fspec[re, lanes], fspec[im, lanes]
            if d < n_dp:
                lanes = pl.ds(d * HALF, HALF)
                more_real, more_imag = sign * fspec[im, lanes], -sign * fspec[re, lanes]
                real = more_real if real is None else real + more_real
                imag = more_imag if imag is None else imag + more_imag
            gspec[d, re, :] = real
            gspec[d, im, :] = imag
        return carry

    lax.fori_loop(0, tiles, combine, 0)

    def transform(distance, keep_lo, keep_hi):
        lo, hi = rbuf[distance, 0], rbuf[distance, 1]
        if keep_lo is not None:
            lo = (lo.astype(F32) * keep_lo).astype(BF16)
            hi = (hi.astype(F32) * keep_hi).astype(BF16)
        both[:, :HALF] = lo
        both[:, HALF:] = hi

        def rows_of(i, carry):
            rows = pl.ds(pl.multiple_of(i * tile, tile), tile)
            spec[distance, rows, :] = jnp.dot(fbuf[rows, :], both[...], preferred_element_type=F32)
            return carry

        lax.fori_loop(0, 4, rows_of, 0)

    def term(d, distance, core, re, im):
        lanes = pl.ds(core * HALF, HALF)
        a, b = gspec[d, re, :], gspec[d, im, :]
        u, v = spec[distance, re, lanes], spec[distance, im, lanes]
        return a * u - b * v, a * v + b * u

    def terms(which, re, im):
        got = [term(d, distance, core, re, im) for d, distance, core in which]
        return sum(g[0] for g in got[1:]) + got[0][0], sum(g[1] for g in got[1:]) + got[0][1]

    for part in (0, 1, 2):
        halo_arrived(0, 1 - c, part)
    transform(0, None, None)
    transform(1, keep2, keep1)

    def early(i, carry):
        re, im = places(i)
        real, imag = terms([(0, 0, 0), (1, 1, 1), (2, 1, 0)], re, im)
        acc[0, re, :] = real
        acc[0, im, :] = imag
        real, imag = terms([(1, 0, 0), (2, 1, 1), (3, 1, 0)], re, im)
        acc[1, re, :] = real
        acc[1, im, :] = imag
        return carry

    lax.fori_loop(0, tiles, early, 0)
    pass_on(2)

    @pl.when(z >= 2)
    def _():
        for part in (0, 1, 2):
            for core in (0, 1):
                halo_arrived(2, core, part)

    transform(2, keep4, keep3)

    def late(i, carry):
        re, im = places(i)
        real, imag = terms([(3, 2, 1), (4, 2, 0)], re, im)
        total[re, pl.ds(0, HALF)] = (acc[0, re, :] + real).astype(BF16)
        total[im, pl.ds(0, HALF)] = (acc[0, im, :] + imag).astype(BF16)
        real, imag = terms([(4, 2, 1)], re, im)
        own_real, own_imag = terms([(0, 0, 1)], re, im)
        total[re, pl.ds(HALF, HALF)] = (own_real + keep_b * (acc[1, re, :] + real)).astype(BF16)
        total[im, pl.ds(HALF, HALF)] = (own_imag + keep_b * (acc[1, im, :] + imag)).astype(BF16)
        return carry

    lax.fori_loop(0, tiles, late, 0)

    loads[3].wait()
    pltpu.make_async_remote_copy(
        src_ref=qsend.at[1 - c], dst_ref=qbuf.at[1 - c], send_sem=q_sem.at[0], recv_sem=q_sem.at[1],
        device_id=sibling, device_id_type=MESH).wait_recv()
    pairs = n_ch // 2
    own_pair = y // 2
    other = y + 1 - 2 * (y % 2)

    def g_copy(to):
        return pltpu.make_async_remote_copy(
            src_ref=gown.at[to], dst_ref=gall.at[y], send_sem=g_send.at[to], recv_sem=g_recv.at[y],
            device_id={"channel": to}, device_id_type=MESH)

    def g_arrived(source):
        pltpu.make_async_remote_copy(
            src_ref=gown.at[source], dst_ref=gall.at[source], send_sem=g_send.at[source], recv_sem=g_recv.at[source],
            device_id={"channel": other}, device_id_type=MESH).wait_recv()

    def f_copy(source):
        return pltpu.make_async_remote_copy(
            src_ref=gall.at[source], dst_ref=gpair.at[source], send_sem=f_send.at[source], recv_sem=f_recv.at[source],
            device_id=partner, device_id_type=MESH)

    for k in range(pairs):
        pair = lax.rem(own_pair + k, pairs)
        rows = pl.ds(pl.multiple_of(pair * 2 * piece, 2 * piece), 2 * piece)
        conv = jnp.dot(ibuf[rows, :], total[...], preferred_element_type=F32)
        for block in (0, 1):
            got = (qbuf[block, rows, :].astype(F32) * conv[:, block * HALF:(block + 1) * HALF]).astype(BF16)
            for i in (0, 1):
                gown[2 * pair + i, pl.ds(block * piece, piece), :] = got[i * piece:(i + 1) * piece]
        if k == 0:
            g_copy(other).start()
            gall[y] = gown[y]
            f_copy(y).start()
        else:
            for i in (0, 1):
                g_copy(2 * pair + i).start()
    pass_on(3)

    def pieces(k):
        pair = lax.rem(own_pair - k + pairs, pairs)
        return 2 * pair, 2 * pair + 1

    def hand_on(k):
        for source in (other,) if k == 0 else pieces(k):
            g_arrived(source)
            f_copy(source).start()

    def tokens(k):
        first, second = pieces(k)
        own = jnp.concatenate([gall[first], gall[second]], 1)
        for source in (first, second):
            f_copy(source).wait_recv()
        return jnp.concatenate([own, jnp.concatenate([gpair[first], gpair[second]], 1)], 0)

    def weights(k, lanes):
        first, second = pieces(k)
        return jnp.concatenate([wall[first, :, lanes], wall[second, :, lanes]], 0)

    def project(k):
        part = jnp.dot(tokens(k), weights(k, slice(None)), preferred_element_type=F32)
        if k == 0:
            osum[...] = part
        else:
            osum[...] += part

    hand_on(0)
    hand_on(1)
    for way in (0, 1):
        w_link(way, w_steps, True)[1].wait_recv()
    m_copy(lax.rem(y + w_steps, n_ch), False).start()
    for by in range(1, n_ch):
        m_copy(lax.rem(y + by, n_ch), True).wait_recv()
    for k in range(pairs - 1):
        project(k)
        if k + 2 < pairs:
            hand_on(k + 2)

    mine = 2 * piece
    part_columns = columns // 2

    def p_copy(whose, h):
        return pltpu.make_async_remote_copy(
            src_ref=psend.at[whose, h], dst_ref=precv.at[whose, h],
            send_sem=p_send.at[whose, h], recv_sem=p_recv.at[whose, h],
            device_id=sibling, device_id_type=MESH)

    def back_copy(h):
        return pltpu.make_async_remote_copy(
            src_ref=rsend.at[h], dst_ref=rrecv.at[h], send_sem=r_send.at[h], recv_sem=r_recv.at[h],
            device_id=partner, device_id_type=MESH)

    def rows_of_block(whose, block):
        return pl.ds(pl.multiple_of(whose * mine + block * piece, piece), piece)

    last = tokens(pairs - 1)
    for h in (0, 1):
        lanes = pl.ds(h * part_columns, part_columns)
        osum[:, lanes] += jnp.dot(last, weights(pairs - 1, lanes), preferred_element_type=F32)
        for whose in (1, 0):
            psend[whose, h] = osum[rows_of_block(whose, 1 - c), lanes].astype(BF16)
            p_copy(whose, h).start()

    def whole(whose, h):
        p_copy(whose, h).wait_recv()
        lanes = pl.ds(h * part_columns, part_columns)
        return (osum[rows_of_block(whose, c), lanes] + precv[whose, h].astype(F32)).astype(BF16)

    def out_lanes(which, h):
        return pl.ds(pl.multiple_of(which * columns + h * part_columns, 128), part_columns)

    for h in (0, 1):
        rsend[h] = whole(1, h)
        back_copy(h).start()
    for h in (0, 1):
        out[:, out_lanes(side, h)] = whole(0, h)
    for h in (0, 1):
        back_copy(h).wait_recv()
        out[:, out_lanes(1 - side, h)] = rrecv[h]

    for h in (0, 1):
        back_copy(h).wait_send()
    q_copy.wait_send()
    for whose in (1, 0):
        for h in (0, 1):
            p_copy(whose, h).wait_send()
    for step in range(1, w_steps + 1):
        for way in (0, 1):
            w_link(way, step, False)[1].wait_send()
    f_copy(y).wait_send()
    for by in range(1, n_ch):
        g_copy(lax.rem(y + by, n_ch)).wait_send()
        m_copy(lax.rem(y + by, n_ch), False).wait_send()
        f_copy(lax.rem(y + by, n_ch)).wait_send()
    @pl.when(ctx + 1 < n_ctx)
    def _():
        tail.wait_send()

    for by in range(1, n_dp):
        tap_copy(by).wait_send()
    each_halo(lambda copy: copy.wait_send(), (0, 1, 2))

    @pl.when((z >= 1) & (z + 1 < chips))
    def _():
        for part in (0, 1, 2):
            for core in (0, 1):
                forward_copy(core, part).wait_send()


def per_device(mesh_shape, features, doc_start, short_taps, long_filter, w_out):
    block_len, channels, d_out = features.shape[1], features.shape[3], w_out.shape[1]
    n_ctx, n_ch, n_dp = mesh_shape["context"], mesh_shape["channel"], mesh_shape["dp"]
    streams = jnp.transpose(features[0], (1, 0, 2))
    forward, inverse = tables(block_len)
    piece, columns = block_len // n_ch, d_out // 2
    width = 2 * block_len
    anywhere = pl.BlockSpec(memory_space=pltpu.HBM)
    vmem = pl.BlockSpec(memory_space=pltpu.VMEM)
    dma = pltpu.SemaphoreType.DMA
    result = pl.pallas_call(
        functools.partial(kernel, (n_ctx, n_ch, n_dp, block_len, d_out)),
        out_shape=jax.ShapeDtypeStruct((piece, d_out), BF16),
        in_specs=[anywhere] * 7,
        out_specs=vmem,
        scratch_shapes=[
            pltpu.SMEM(doc_start.shape, jnp.int32),
            pltpu.VMEM(short_taps.shape, F32),
            pltpu.VMEM((3, 16 + block_len, channels), BF16),
            pltpu.VMEM((width, block_len), BF16),
            pltpu.VMEM((block_len, width), BF16),
            pltpu.VMEM((n_ch, HALF, columns), BF16),
            pltpu.VMEM((2, block_len, HALF), BF16),
            pltpu.VMEM((3, 2, block_len, HALF), BF16),
            pltpu.VMEM((n_dp, HALF, block_len), BF16),
            pltpu.VMEM((block_len, 2 * HALF), BF16),
            pltpu.VMEM((width, n_dp * HALF), F32),
            pltpu.VMEM((n_dp + 1, width, HALF), F32),
            pltpu.VMEM((3, width, 2 * HALF), F32),
            pltpu.VMEM((2, block_len, HALF), BF16),
            pltpu.VMEM((2, block_len, HALF), BF16),
            pltpu.VMEM((2, width, HALF), F32),
            pltpu.VMEM((width, 2 * HALF), BF16),
            pltpu.VMEM((n_ch, 2 * piece, HALF), BF16),
            pltpu.VMEM((n_ch, 2 * piece, HALF), BF16),
            pltpu.VMEM((n_ch, 2 * piece, HALF), BF16),
            pltpu.VMEM((4 * piece, columns), F32),
            pltpu.VMEM((2, 2, piece, columns // 2), BF16),
            pltpu.VMEM((2, 2, piece, columns // 2), BF16),
            pltpu.VMEM((2, piece, columns // 2), BF16),
            pltpu.VMEM((2, piece, columns // 2), BF16),
            dma((7,)), dma((2,)), dma((n_dp - 1,)), dma((n_dp - 1,)), dma((3, 2, 3)), dma((3, 2, 3)), dma((2,)),
            dma((2, n_ch // 2)), dma((2, n_ch // 2)), dma((n_ch,)), dma((n_ch,)), dma((n_ch,)), dma((n_ch,)), dma((n_ch,)), dma((n_ch,)),
            dma((2, 2)), dma((2, 2)), dma((2,)), dma((2,)),
        ],
        compiler_params=pltpu.CompilerParams(
            collective_id=0, has_side_effects=True, vmem_limit_bytes=60 * 1024 * 1024),
    )(doc_start, short_taps, streams, long_filter, w_out, forward, inverse)
    return result[None]


def solution(mesh):
    return jax.shard_map(
        functools.partial(per_device, dict(mesh.shape)),
        mesh=mesh,
        in_specs=(
            P("dp", "context", None, "channel"),
            P("dp", None),
            P(None, None, "channel"),
            P("channel", "dp"),
            P("channel", None),
        ),
        out_specs=P("dp", ("context", "channel"), None),
        check_vma=False,
    )
```

```python
import functools

import jax
import jax.numpy as jnp
import numpy as np
from jax import lax
from jax.experimental import pallas as pl
from jax.experimental.pallas import tpu as pltpu
from jax.sharding import PartitionSpec as P

MESH = pl.DeviceIdType.MESH
F32 = jnp.float32
BF16 = jnp.bfloat16
HALF = 128


def tables(block_len):
    freq = np.concatenate([np.arange(0, block_len, 2), np.arange(1, block_len, 2)])
    angle = 2.0 * np.pi * ((2 * freq[:, None] + 1) * np.arange(block_len)[None, :] % (4 * block_len)) / (4 * block_len)
    sign = np.where(freq % 2 == 0, 1.0, -1.0)[:, None]
    forward = np.concatenate([np.cos(angle), -np.sin(angle)], 0)
    inverse = np.concatenate([-sign * np.sin(angle), -sign * np.cos(angle)], 0).T / block_len
    return forward.astype(jnp.bfloat16), inverse.astype(jnp.bfloat16)


def kernel(
    sizes, doc_in, taps_in, x, filt, w, fwd, inv, out,
    doc, taps, ext, fbuf, ibuf, wall, pbuf, rbuf, tbuf, both, fspec, gspec, spec, qbuf, qsend, acc, total,
    gown, gall, gpair, osum, psend, precv, rsend, rrecv,
    load_sem, tail_sem, tap_send, tap_recv, halo_send, halo_recv, q_sem, w_send, w_recv, e_send, e_recv, m_send, m_recv, u_send, u_recv,
    g_send, g_recv, f_send, f_recv, p_send, p_recv, r_send, r_recv,
):
    n_ctx, n_ch, n_dp, block_len, d_out = sizes
    chips = n_ctx // 2
    ctx = lax.axis_index("context")
    y = lax.axis_index("channel")
    xi = lax.axis_index("dp")
    z = ctx // 2
    c = ctx % 2
    piece = block_len // n_ch
    columns = d_out // 2
    sibling = {"context": 2 * z + 1 - c}
    odd = xi % 2
    side = ((xi + 1) // 2) % 2
    partner = {"dp": xi + 1 - 2 * odd}
    mate = {"dp": lax.rem(xi + 2 * odd - 1 + n_dp, n_dp)}

    def chip(distance):
        return lax.rem(z + distance + chips, chips)

    barrier = pltpu.get_barrier_semaphore()
    pl.semaphore_signal(barrier, inc=1, device_id=sibling, device_id_type=MESH)

    @pl.when(z >= 1)
    def _():
        for core in (0, 1):
            pl.semaphore_signal(barrier, inc=1, device_id={"context": 2 * chip(-1) + core}, device_id_type=MESH)

    @pl.when(z + 1 < chips)
    def _():
        pl.semaphore_signal(barrier, inc=1, device_id={"context": 2 * chip(1) + c}, device_id_type=MESH)

    for by in range(1, n_dp):
        pl.semaphore_signal(barrier, inc=1, device_id={"dp": lax.rem(xi + by, n_dp)}, device_id_type=MESH)
    for by in range(1, n_ch):
        pl.semaphore_signal(barrier, inc=1, device_id={"channel": lax.rem(y + by, n_ch)}, device_id_type=MESH)

    own_rows = pl.ds(pl.multiple_of(c * HALF, HALF), HALF)
    loads = [
        pltpu.make_async_copy(x, ext.at[:, pl.ds(16, block_len), :], load_sem.at[0]),
        pltpu.make_async_copy(filt.at[own_rows, :], tbuf.at[xi], load_sem.at[1]),
        pltpu.make_async_copy(fwd, fbuf, load_sem.at[2]),
        pltpu.make_async_copy(inv, ibuf, load_sem.at[3]),
        pltpu.make_async_copy(
            w.at[own_rows, pl.ds(pl.multiple_of(side * columns, 128), columns)], wall.at[y], load_sem.at[4]),
        pltpu.make_async_copy(doc_in, doc, load_sem.at[5]),
        pltpu.make_async_copy(taps_in, taps, load_sem.at[6]),
    ]
    for load in loads:
        load.start()
    def tap_copy(by):
        return pltpu.make_async_remote_copy(
            src_ref=filt.at[own_rows, :], dst_ref=tbuf.at[xi],
            send_sem=tap_send.at[by - 1], recv_sem=tap_recv.at[by - 1],
            device_id={"dp": lax.rem(xi + by, n_dp)}, device_id_type=MESH)

    loads[5].wait()
    loads[6].wait()

    def goes_on(block):
        at = jnp.maximum(block, 0)
        return jnp.where((block > 0) & (doc[0, at] != 1), 1.0, 0.0).astype(F32)

    own_goes_on = goes_on(ctx)
    keep_b = goes_on(2 * z + 1)
    keep1 = goes_on(2 * z)
    keep2 = keep1 * goes_on(2 * z - 1)
    keep3 = keep2 * goes_on(2 * z - 2)
    keep4 = keep3 * goes_on(2 * z - 3)

    chunk = min(128, block_len)

    def smooth(stream, start, count):
        rows = ext[stream, pl.ds(start, count + 16), :].astype(F32)
        got = (
            taps[0, pl.ds(stream, 1), :] * rows
            + taps[1, pl.ds(stream, 1), :] * pltpu.roll(rows, 1, 0)
            + taps[2, pl.ds(stream, 1), :] * pltpu.roll(rows, 2, 0)
        )
        return got[16:]

    def make_product(start, count):
        product = (smooth(1, start, count) * smooth(2, start, count)).astype(BF16)
        pbuf[0, pl.ds(start, count), :] = product[:, :HALF]
        pbuf[1, pl.ds(start, count), :] = product[:, HALF:]

    def make_gate(start, count):
        smoothed = smooth(0, start, count).astype(BF16)
        qsend[0, pl.ds(start, count), :] = smoothed[:, :HALF]
        qsend[1, pl.ds(start, count), :] = smoothed[:, HALF:]

    middle = block_len // 2
    parts = (pl.ds(16, middle - 16), pl.ds(middle, middle), pl.ds(0, 16))

    def halo_copy(distance, half, part):
        return pltpu.make_async_remote_copy(
            src_ref=pbuf.at[half, parts[part], :], dst_ref=rbuf.at[distance, c, parts[part], :],
            send_sem=halo_send.at[distance, half, part], recv_sem=halo_recv.at[distance, c, part],
            device_id={"context": 2 * chip(distance) + half}, device_id_type=MESH)

    def forward_copy(core, part):
        return pltpu.make_async_remote_copy(
            src_ref=rbuf.at[1, core, parts[part], :], dst_ref=rbuf.at[2, core, parts[part], :],
            send_sem=halo_send.at[2, core, part], recv_sem=halo_recv.at[2, core, part],
            device_id={"context": 2 * chip(1) + c}, device_id_type=MESH)

    def halo_arrived(distance, core, part):
        pltpu.make_async_remote_copy(
            src_ref=pbuf.at[0, parts[part], :], dst_ref=rbuf.at[distance, core, parts[part], :],
            send_sem=halo_send.at[distance, 0, part], recv_sem=halo_recv.at[distance, core, part],
            device_id=sibling, device_id_type=MESH).wait_recv()

    def each_halo(act, parts_of):
        @pl.when(z + 1 < chips)
        def _():
            for part in parts_of:
                for half in (0, 1):
                    act(halo_copy(1, half, part))

        for part in parts_of:
            act(halo_copy(0, 1 - c, part))

    def take_in(parts_of):
        @pl.when(z >= 1)
        def _():
            for part in parts_of:
                for core in (0, 1):
                    halo_arrived(1, core, part)

        @pl.when((z >= 1) & (z + 1 < chips))
        def _():
            for part in parts_of:
                for core in (0, 1):
                    forward_copy(core, part).start()

    def make_products(lo, hi):
        for start in range(lo, hi, chunk):
            first = max(start, 16)
            make_product(first, start + chunk - first)

    loads[0].wait()
    make_products(0, 0 * chunk)
    ahead = jnp.where(z + 1 < chips, 2, 0) + jnp.where(z >= 1, 1, 0)
    pl.semaphore_wait(barrier, 1 + ahead + (n_dp - 1) + (n_ch - 1))

    tail = pltpu.make_async_remote_copy(
        src_ref=x.at[:, pl.ds(block_len - 16, 16), :], dst_ref=ext.at[:, pl.ds(0, 16), :],
        send_sem=tail_sem.at[0], recv_sem=tail_sem.at[1],
        device_id={"context": lax.rem(ctx + 1, n_ctx)}, device_id_type=MESH)

    @pl.when(ctx + 1 < n_ctx)
    def _():
        tail.start()


    w_steps = n_ch // 2

    quarter = columns // 4

    level = z % 2
    half_of = (odd + level) % 2
    given = 2 * half_of + level
    from_mate = 2 * (1 - half_of) + level
    from_next = 2 * (1 - half_of) + 1 - level

    def ring_link(way, step, arriving, start, count, send, recv):
        by = (1, n_ch - 1)[way]
        source = lax.rem(y + (n_ch - by) * (step if arriving else step - 1), n_ch)
        if step == w_steps:
            count = count // 2
            start = start + way * count
        lanes = pl.ds(pl.multiple_of(start, 128), count)
        return source, pltpu.make_async_remote_copy(
            src_ref=wall.at[source, :, lanes], dst_ref=wall.at[source, :, lanes],
            send_sem=send.at[way, step - 1], recv_sem=recv.at[way, step - 1],
            device_id={"channel": lax.rem(y + by, n_ch)}, device_id_type=MESH)

    def w_link(way, step, arriving):
        return ring_link(way, step, arriving, half_of * 2 * quarter, 2 * quarter, w_send, w_recv)

    def e_link(way, step, arriving):
        return ring_link(way, step, arriving, from_next * quarter, quarter, e_send, e_recv)

    def quarter_copy(source, place, send, recv, to):
        lanes = pl.ds(pl.multiple_of(place * quarter, 128), quarter)
        return pltpu.make_async_remote_copy(
            src_ref=wall.at[source, :, lanes], dst_ref=wall.at[source, :, lanes],
            send_sem=send.at[source], recv_sem=recv.at[source], device_id=to, device_id_type=MESH)

    def m_copy(source, arriving):
        return quarter_copy(source, from_mate if arriving else given, m_send, m_recv, mate)

    def u_copy(source, arriving):
        return quarter_copy(
            source, from_next if arriving else given, u_send, u_recv, {"context": 2 * chip(-1) + c})

    def give(source):
        m_copy(source, False).start()

        @pl.when(z >= 1)
        def _():
            u_copy(source, False).start()

    def pass_on(step):
        if step < w_steps:
            for way in (0, 1):
                source, arrival = w_link(way, step, True)
                arrival.wait_recv()
                w_link(way, step + 1, False)[1].start()
                give(source)

            @pl.when(z + 1 == chips)
            def _():
                for way in (0, 1):
                    e_link(way, step, True)[1].wait_recv()
                    e_link(way, step + 1, False)[1].start()

    loads[4].wait()
    for way in (0, 1):
        w_link(way, 1, False)[1].start()

    @pl.when(z + 1 == chips)
    def _():
        for way in (0, 1):
            e_link(way, 1, False)[1].start()

    for by in range(1, n_dp):
        tap_copy(by).start()

    make_products(0 * chunk, block_len)
    each_halo(lambda copy: copy.start(), (0, 1))

    for start in range(0, block_len, chunk):
        first = max(start, 16)
        make_gate(first, start + chunk - first)
    for distance in (1, 2):
        @pl.when(z < distance)
        def _():
            rbuf[distance] = jnp.zeros(rbuf.shape[1:], BF16)

    @pl.when(ctx > 0)
    def _():
        tail.wait_recv()

    @pl.when(ctx == 0)
    def _():
        ext[:, pl.ds(0, 16), :] = jnp.zeros((3, 16, ext.shape[2]), BF16)

    for stream in range(3):
        ext[stream, pl.ds(0, 16), :] = (ext[stream, pl.ds(0, 16), :].astype(F32) * own_goes_on).astype(BF16)
    make_product(0, 16)
    each_halo(lambda copy: copy.start(), (2,))
    make_gate(0, 16)
    q_copy = pltpu.make_async_remote_copy(
        src_ref=qsend.at[1 - c], dst_ref=qbuf.at[c], send_sem=q_sem.at[0], recv_sem=q_sem.at[1],
        device_id=sibling, device_id_type=MESH)
    q_copy.start()
    qbuf[c] = qsend[c]
    rbuf[0, c] = pbuf[c]

    pass_on(1)

    loads[1].wait()
    loads[2].wait()
    for by in range(1, n_dp):
        tap_copy(by).wait_recv()
    tile = block_len // 2

    def filter_rows(i, carry):
        rows = pl.ds(pl.multiple_of(i * tile, tile), tile)
        fspec[rows, :] = lax.dot_general(
            fbuf[rows, :], tbuf[...].reshape(n_dp * HALF, block_len), (((1,), (1,)), ((), ())), preferred_element_type=F32)
        return carry

    take_in((0,))
    lax.fori_loop(0, 4, filter_rows, 0)
    take_in((1, 2))
    pass_on(2)

    step_rows = min(64, block_len // 2)
    tiles = block_len // step_rows

    def places(i):
        at = pl.multiple_of(i * step_rows, step_rows)
        return pl.ds(at, step_rows), pl.ds(block_len + at, step_rows)

    def combine(i, carry):
        re, im = places(i)
        sign = (1 - 2 * (i // (tiles // 2))).astype(F32)
        for d in range(n_dp + 1):
            real = imag = None
            if d > 0:
                lanes = pl.ds((d - 1) * HALF, HALF)
                real, imag = fspec[re, lanes], fspec[im, lanes]
            if d < n_dp:
                lanes = pl.ds(d * HALF, HALF)
                more_real, more_imag = sign * fspec[im, lanes], -sign * fspec[re, lanes]
                real = more_real if real is None else real + more_real
                imag = more_imag if imag is None else imag + more_imag
            gspec[d, re, :] = real
            gspec[d, im, :] = imag
        return carry

    lax.fori_loop(0, tiles, combine, 0)

    def transform(distance, keep_lo, keep_hi):
        lo, hi = rbuf[distance, 0], rbuf[distance, 1]
        if keep_lo is not None:
            lo = (lo.astype(F32) * keep_lo).astype(BF16)
            hi = (hi.astype(F32) * keep_hi).astype(BF16)
        both[:, :HALF] = lo
        both[:, HALF:] = hi

        def rows_of(i, carry):
            rows = pl.ds(pl.multiple_of(i * tile, tile), tile)
            spec[distance, rows, :] = jnp.dot(fbuf[rows, :], both[...], preferred_element_type=F32)
            return carry

        lax.fori_loop(0, 4, rows_of, 0)

    def term(d, distance, core, re, im):
        lanes = pl.ds(core * HALF, HALF)
        a, b = gspec[d, re, :], gspec[d, im, :]
        u, v = spec[distance, re, lanes], spec[distance, im, lanes]
        return a * u - b * v, a * v + b * u

    def terms(which, re, im):
        got = [term(d, distance, core, re, im) for d, distance, core in which]
        return sum(g[0] for g in got[1:]) + got[0][0], sum(g[1] for g in got[1:]) + got[0][1]

    for part in (0, 1, 2):
        halo_arrived(0, 1 - c, part)
    transform(0, None, None)
    transform(1, keep2, keep1)

    def early(i, carry):
        re, im = places(i)
        real, imag = terms([(0, 0, 0), (1, 1, 1), (2, 1, 0)], re, im)
        acc[0, re, :] = real
        acc[0, im, :] = imag
        real, imag = terms([(1, 0, 0), (2, 1, 1), (3, 1, 0)], re, im)
        acc[1, re, :] = real
        acc[1, im, :] = imag
        return carry

    lax.fori_loop(0, tiles, early, 0)
    pass_on(3)

    @pl.when(z >= 2)
    def _():
        for part in (0, 1, 2):
            for core in (0, 1):
                halo_arrived(2, core, part)

    transform(2, keep4, keep3)

    def late(i, carry):
        re, im = places(i)
        real, imag = terms([(3, 2, 1), (4, 2, 0)], re, im)
        total[re, pl.ds(0, HALF)] = (acc[0, re, :] + real).astype(BF16)
        total[im, pl.ds(0, HALF)] = (acc[0, im, :] + imag).astype(BF16)
        real, imag = terms([(4, 2, 1)], re, im)
        own_real, own_imag = terms([(0, 0, 1)], re, im)
        total[re, pl.ds(HALF, HALF)] = (own_real + keep_b * (acc[1, re, :] + real)).astype(BF16)
        total[im, pl.ds(HALF, HALF)] = (own_imag + keep_b * (acc[1, im, :] + imag)).astype(BF16)
        return carry

    lax.fori_loop(0, tiles, late, 0)

    loads[3].wait()
    pltpu.make_async_remote_copy(
        src_ref=qsend.at[1 - c], dst_ref=qbuf.at[1 - c], send_sem=q_sem.at[0], recv_sem=q_sem.at[1],
        device_id=sibling, device_id_type=MESH).wait_recv()
    pairs = n_ch // 2
    own_pair = y // 2
    other = y + 1 - 2 * (y % 2)

    def g_copy(to):
        return pltpu.make_async_remote_copy(
            src_ref=gown.at[to], dst_ref=gall.at[y], send_sem=g_send.at[to], recv_sem=g_recv.at[y],
            device_id={"channel": to}, device_id_type=MESH)

    def g_arrived(source):
        pltpu.make_async_remote_copy(
            src_ref=gown.at[source], dst_ref=gall.at[source], send_sem=g_send.at[source], recv_sem=g_recv.at[source],
            device_id={"channel": other}, device_id_type=MESH).wait_recv()

    def f_copy(source):
        return pltpu.make_async_remote_copy(
            src_ref=gall.at[source], dst_ref=gpair.at[source], send_sem=f_send.at[source], recv_sem=f_recv.at[source],
            device_id=partner, device_id_type=MESH)

    for k in range(pairs):
        pair = lax.rem(own_pair + k, pairs)
        rows = pl.ds(pl.multiple_of(pair * 2 * piece, 2 * piece), 2 * piece)
        conv = jnp.dot(ibuf[rows, :], total[...], preferred_element_type=F32)
        for block in (0, 1):
            got = (qbuf[block, rows, :].astype(F32) * conv[:, block * HALF:(block + 1) * HALF]).astype(BF16)
            for i in (0, 1):
                gown[2 * pair + i, pl.ds(block * piece, piece), :] = got[i * piece:(i + 1) * piece]
        if k == 0:
            g_copy(other).start()
            gall[y] = gown[y]
            f_copy(y).start()
        else:
            for i in (0, 1):
                g_copy(2 * pair + i).start()

    for way in (0, 1):
        w_link(way, w_steps, True)[1].wait_recv()
    give(lax.rem(y + w_steps, n_ch))

    def pieces(k):
        pair = lax.rem(own_pair - k + pairs, pairs)
        return 2 * pair, 2 * pair + 1

    def hand_on(k):
        for source in (other,) if k == 0 else pieces(k):
            g_arrived(source)
            f_copy(source).start()

    def tokens(k):
        first, second = pieces(k)
        own = jnp.concatenate([gall[first], gall[second]], 1)
        for source in (first, second):
            f_copy(source).wait_recv()
        return jnp.concatenate([own, jnp.concatenate([gpair[first], gpair[second]], 1)], 0)

    def weights(k, lanes):
        first, second = pieces(k)
        return jnp.concatenate([wall[first, :, lanes], wall[second, :, lanes]], 0)

    def project(k):
        part = jnp.dot(tokens(k), weights(k, slice(None)), preferred_element_type=F32)
        if k == 0:
            osum[...] = part
        else:
            osum[...] += part

    hand_on(0)
    hand_on(1)
    hand_on(2)
    for by in range(1, n_ch):
        m_copy(lax.rem(y + by, n_ch), True).wait_recv()

    @pl.when(z + 1 < chips)
    def _():
        for by in range(1, n_ch):
            u_copy(lax.rem(y + by, n_ch), True).wait_recv()

    @pl.when(z + 1 == chips)
    def _():
        for way in (0, 1):
            e_link(way, w_steps, True)[1].wait_recv()

    for k in range(pairs - 1):
        project(k)
        if k + 3 < pairs:
            hand_on(k + 3)

    mine = 2 * piece
    part_columns = columns // 2

    def p_copy(whose, h):
        return pltpu.make_async_remote_copy(
            src_ref=psend.at[whose, h], dst_ref=precv.at[whose, h],
            send_sem=p_send.at[whose, h], recv_sem=p_recv.at[whose, h],
            device_id=sibling, device_id_type=MESH)

    def back_copy(h):
        return pltpu.make_async_remote_copy(
            src_ref=rsend.at[h], dst_ref=rrecv.at[h], send_sem=r_send.at[h], recv_sem=r_recv.at[h],
            device_id=partner, device_id_type=MESH)

    def rows_of_block(whose, block):
        return pl.ds(pl.multiple_of(whose * mine + block * piece, piece), piece)

    last = tokens(pairs - 1)
    for h in (0, 1):
        lanes = pl.ds(h * part_columns, part_columns)
        osum[:, lanes] += jnp.dot(last, weights(pairs - 1, lanes), preferred_element_type=F32)
        for whose in (1, 0):
            psend[whose, h] = osum[rows_of_block(whose, 1 - c), lanes].astype(BF16)
            p_copy(whose, h).start()

    def whole(whose, h):
        p_copy(whose, h).wait_recv()
        lanes = pl.ds(h * part_columns, part_columns)
        return (osum[rows_of_block(whose, c), lanes] + precv[whose, h].astype(F32)).astype(BF16)

    def out_lanes(which, h):
        return pl.ds(pl.multiple_of(which * columns + h * part_columns, 128), part_columns)

    for h in (0, 1):
        rsend[h] = whole(1, h)
        back_copy(h).start()
    for h in (0, 1):
        out[:, out_lanes(side, h)] = whole(0, h)
    for h in (0, 1):
        back_copy(h).wait_recv()
        out[:, out_lanes(1 - side, h)] = rrecv[h]

    for h in (0, 1):
        back_copy(h).wait_send()
    q_copy.wait_send()
    for whose in (1, 0):
        for h in (0, 1):
            p_copy(whose, h).wait_send()
    for step in range(1, w_steps + 1):
        for way in (0, 1):
            w_link(way, step, False)[1].wait_send()
    f_copy(y).wait_send()

    @pl.when(z >= 1)
    def _():
        for by in range(1, n_ch):
            u_copy(lax.rem(y + by, n_ch), False).wait_send()

    @pl.when(z + 1 == chips)
    def _():
        for step in range(1, w_steps + 1):
            for way in (0, 1):
                e_link(way, step, False)[1].wait_send()

    for by in range(1, n_ch):
        g_copy(lax.rem(y + by, n_ch)).wait_send()
        m_copy(lax.rem(y + by, n_ch), False).wait_send()
        f_copy(lax.rem(y + by, n_ch)).wait_send()
    @pl.when(ctx + 1 < n_ctx)
    def _():
        tail.wait_send()

    for by in range(1, n_dp):
        tap_copy(by).wait_send()
    each_halo(lambda copy: copy.wait_send(), (0, 1, 2))

    @pl.when((z >= 1) & (z + 1 < chips))
    def _():
        for part in (0, 1, 2):
            for core in (0, 1):
                forward_copy(core, part).wait_send()


def per_device(mesh_shape, features, doc_start, short_taps, long_filter, w_out):
    block_len, channels, d_out = features.shape[1], features.shape[3], w_out.shape[1]
    n_ctx, n_ch, n_dp = mesh_shape["context"], mesh_shape["channel"], mesh_shape["dp"]
    streams = jnp.transpose(features[0], (1, 0, 2))
    forward, inverse = tables(block_len)
    piece, columns = block_len // n_ch, d_out // 2
    width = 2 * block_len
    anywhere = pl.BlockSpec(memory_space=pltpu.HBM)
    vmem = pl.BlockSpec(memory_space=pltpu.VMEM)
    dma = pltpu.SemaphoreType.DMA
    result = pl.pallas_call(
        functools.partial(kernel, (n_ctx, n_ch, n_dp, block_len, d_out)),
        out_shape=jax.ShapeDtypeStruct((piece, d_out), BF16),
        in_specs=[anywhere] * 7,
        out_specs=vmem,
        scratch_shapes=[
            pltpu.SMEM(doc_start.shape, jnp.int32),
            pltpu.VMEM(short_taps.shape, F32),
            pltpu.VMEM((3, 16 + block_len, channels), BF16),
            pltpu.VMEM((width, block_len), BF16),
            pltpu.VMEM((block_len, width), BF16),
            pltpu.VMEM((n_ch, HALF, columns), BF16),
            pltpu.VMEM((2, block_len, HALF), BF16),
            pltpu.VMEM((3, 2, block_len, HALF), BF16),
            pltpu.VMEM((n_dp, HALF, block_len), BF16),
            pltpu.VMEM((block_len, 2 * HALF), BF16),
            pltpu.VMEM((width, n_dp * HALF), F32),
            pltpu.VMEM((n_dp + 1, width, HALF), F32),
            pltpu.VMEM((3, width, 2 * HALF), F32),
            pltpu.VMEM((2, block_len, HALF), BF16),
            pltpu.VMEM((2, block_len, HALF), BF16),
            pltpu.VMEM((2, width, HALF), F32),
            pltpu.VMEM((width, 2 * HALF), BF16),
            pltpu.VMEM((n_ch, 2 * piece, HALF), BF16),
            pltpu.VMEM((n_ch, 2 * piece, HALF), BF16),
            pltpu.VMEM((n_ch, 2 * piece, HALF), BF16),
            pltpu.VMEM((4 * piece, columns), F32),
            pltpu.VMEM((2, 2, piece, columns // 2), BF16),
            pltpu.VMEM((2, 2, piece, columns // 2), BF16),
            pltpu.VMEM((2, piece, columns // 2), BF16),
            pltpu.VMEM((2, piece, columns // 2), BF16),
            dma((7,)), dma((2,)), dma((n_dp - 1,)), dma((n_dp - 1,)), dma((3, 2, 3)), dma((3, 2, 3)), dma((2,)),
            dma((2, n_ch // 2)), dma((2, n_ch // 2)), dma((2, n_ch // 2)), dma((2, n_ch // 2)),
            dma((n_ch,)), dma((n_ch,)), dma((n_ch,)), dma((n_ch,)), dma((n_ch,)), dma((n_ch,)), dma((n_ch,)), dma((n_ch,)),
            dma((2, 2)), dma((2, 2)), dma((2,)), dma((2,)),
        ],
        compiler_params=pltpu.CompilerParams(
            collective_id=0, has_side_effects=True, vmem_limit_bytes=60 * 1024 * 1024),
    )(doc_start, short_taps, streams, long_filter, w_out, forward, inverse)
    return result[None]


def solution(mesh):
    return jax.shard_map(
        functools.partial(per_device, dict(mesh.shape)),
        mesh=mesh,
        in_specs=(
            P("dp", "context", None, "channel"),
            P("dp", None),
            P(None, None, "channel"),
            P("channel", "dp"),
            P("channel", None),
        ),
        out_specs=P("dp", ("context", "channel"), None),
        check_vma=False,
    )
```

```python
import functools

import jax
import jax.numpy as jnp
import numpy as np
from jax import lax
from jax.experimental import pallas as pl
from jax.experimental.pallas import tpu as pltpu
from jax.sharding import PartitionSpec as P

MESH = pl.DeviceIdType.MESH
F32 = jnp.float32
BF16 = jnp.bfloat16
HALF = 128


def tables(block_len):
    freq = np.concatenate([np.arange(0, block_len, 2), np.arange(1, block_len, 2)])
    angle = 2.0 * np.pi * ((2 * freq[:, None] + 1) * np.arange(block_len)[None, :] % (4 * block_len)) / (4 * block_len)
    sign = np.where(freq % 2 == 0, 1.0, -1.0)[:, None]
    forward = np.concatenate([np.cos(angle), -np.sin(angle)], 0)
    inverse = np.concatenate([-sign * np.sin(angle), -sign * np.cos(angle)], 0).T / block_len
    return forward.astype(jnp.bfloat16), inverse.astype(jnp.bfloat16)


def kernel(
    sizes, doc_in, taps_in, x, filt, w, fwd, inv, out,
    doc, taps, ext, fbuf, ibuf, wall, pbuf, rbuf, tbuf, both, fspec, gspec, spec, qbuf, qsend, acc, total,
    gown, gall, gpair, osum, psend, precv, rsend, rrecv,
    load_sem, tail_sem, tap_send, tap_recv, halo_send, halo_recv, q_sem, w_send, w_recv, e_send, e_recv, m_send, m_recv, u_send, u_recv,
    g_send, g_recv, f_send, f_recv, p_send, p_recv, r_send, r_recv,
):
    n_ctx, n_ch, n_dp, block_len, d_out = sizes
    chips = n_ctx // 2
    ctx = lax.axis_index("context")
    y = lax.axis_index("channel")
    xi = lax.axis_index("dp")
    z = ctx // 2
    c = ctx % 2
    piece = block_len // n_ch
    columns = d_out // 2
    sibling = {"context": 2 * z + 1 - c}
    odd = xi % 2
    side = ((xi + 1) // 2) % 2
    partner = {"dp": xi + 1 - 2 * odd}
    mate = {"dp": lax.rem(xi + 2 * odd - 1 + n_dp, n_dp)}

    def chip(distance):
        return lax.rem(z + distance + chips, chips)

    barrier = pltpu.get_barrier_semaphore()
    pl.semaphore_signal(barrier, inc=1, device_id=sibling, device_id_type=MESH)

    @pl.when(z >= 1)
    def _():
        for core in (0, 1):
            pl.semaphore_signal(barrier, inc=1, device_id={"context": 2 * chip(-1) + core}, device_id_type=MESH)

    @pl.when(z + 1 < chips)
    def _():
        pl.semaphore_signal(barrier, inc=1, device_id={"context": 2 * chip(1) + c}, device_id_type=MESH)

    for by in range(1, n_dp):
        pl.semaphore_signal(barrier, inc=1, device_id={"dp": lax.rem(xi + by, n_dp)}, device_id_type=MESH)
    for by in range(1, n_ch):
        pl.semaphore_signal(barrier, inc=1, device_id={"channel": lax.rem(y + by, n_ch)}, device_id_type=MESH)

    own_rows = pl.ds(pl.multiple_of(c * HALF, HALF), HALF)
    loads = [
        pltpu.make_async_copy(x, ext.at[:, pl.ds(16, block_len), :], load_sem.at[0]),
        pltpu.make_async_copy(filt.at[own_rows, :], tbuf.at[xi], load_sem.at[1]),
        pltpu.make_async_copy(fwd, fbuf, load_sem.at[2]),
        pltpu.make_async_copy(inv, ibuf, load_sem.at[3]),
        pltpu.make_async_copy(
            w.at[own_rows, pl.ds(pl.multiple_of(side * columns, 128), columns)], wall.at[y], load_sem.at[4]),
        pltpu.make_async_copy(doc_in, doc, load_sem.at[5]),
        pltpu.make_async_copy(taps_in, taps, load_sem.at[6]),
    ]
    for load in loads:
        load.start()
    def tap_copy(by):
        return pltpu.make_async_remote_copy(
            src_ref=filt.at[own_rows, :], dst_ref=tbuf.at[xi],
            send_sem=tap_send.at[by - 1], recv_sem=tap_recv.at[by - 1],
            device_id={"dp": lax.rem(xi + by, n_dp)}, device_id_type=MESH)

    loads[5].wait()
    loads[6].wait()

    def goes_on(block):
        at = jnp.maximum(block, 0)
        return jnp.where((block > 0) & (doc[0, at] != 1), 1.0, 0.0).astype(F32)

    own_goes_on = goes_on(ctx)
    keep_b = goes_on(2 * z + 1)
    keep1 = goes_on(2 * z)
    keep2 = keep1 * goes_on(2 * z - 1)
    keep3 = keep2 * goes_on(2 * z - 2)
    keep4 = keep3 * goes_on(2 * z - 3)

    chunk = min(128, block_len)

    def smooth(stream, start, count):
        rows = ext[stream, pl.ds(start, count + 16), :].astype(F32)
        got = (
            taps[0, pl.ds(stream, 1), :] * rows
            + taps[1, pl.ds(stream, 1), :] * pltpu.roll(rows, 1, 0)
            + taps[2, pl.ds(stream, 1), :] * pltpu.roll(rows, 2, 0)
        )
        return got[16:]

    def make_product(start, count):
        product = (smooth(1, start, count) * smooth(2, start, count)).astype(BF16)
        pbuf[0, pl.ds(start, count), :] = product[:, :HALF]
        pbuf[1, pl.ds(start, count), :] = product[:, HALF:]

    def make_gate(start, count):
        smoothed = smooth(0, start, count).astype(BF16)
        qsend[0, pl.ds(start, count), :] = smoothed[:, :HALF]
        qsend[1, pl.ds(start, count), :] = smoothed[:, HALF:]

    middle = block_len // 2
    parts = (pl.ds(16, middle - 16), pl.ds(middle, middle), pl.ds(0, 16))

    def halo_copy(distance, half, part):
        return pltpu.make_async_remote_copy(
            src_ref=pbuf.at[half, parts[part], :], dst_ref=rbuf.at[distance, c, parts[part], :],
            send_sem=halo_send.at[distance, half, part], recv_sem=halo_recv.at[distance, c, part],
            device_id={"context": 2 * chip(distance) + half}, device_id_type=MESH)

    def forward_copy(core, part):
        return pltpu.make_async_remote_copy(
            src_ref=rbuf.at[1, core, parts[part], :], dst_ref=rbuf.at[2, core, parts[part], :],
            send_sem=halo_send.at[2, core, part], recv_sem=halo_recv.at[2, core, part],
            device_id={"context": 2 * chip(1) + c}, device_id_type=MESH)

    def halo_arrived(distance, core, part):
        pltpu.make_async_remote_copy(
            src_ref=pbuf.at[0, parts[part], :], dst_ref=rbuf.at[distance, core, parts[part], :],
            send_sem=halo_send.at[distance, 0, part], recv_sem=halo_recv.at[distance, core, part],
            device_id=sibling, device_id_type=MESH).wait_recv()

    def each_halo(act, parts_of):
        @pl.when(z + 1 < chips)
        def _():
            for part in parts_of:
                for half in (0, 1):
                    act(halo_copy(1, half, part))

        for part in parts_of:
            act(halo_copy(0, 1 - c, part))

    def take_in(parts_of):
        @pl.when(z >= 1)
        def _():
            for part in parts_of:
                for core in (0, 1):
                    halo_arrived(1, core, part)

        @pl.when((z >= 1) & (z + 1 < chips))
        def _():
            for part in parts_of:
                for core in (0, 1):
                    forward_copy(core, part).start()

    def make_products(lo, hi):
        for start in range(lo, hi, chunk):
            first = max(start, 16)
            make_product(first, start + chunk - first)

    loads[0].wait()
    make_products(0, block_len)
    for start in range(0, block_len, chunk):
        first = max(start, 16)
        make_gate(first, start + chunk - first)
    ahead = jnp.where(z + 1 < chips, 2, 0) + jnp.where(z >= 1, 1, 0)
    pl.semaphore_wait(barrier, 1 + ahead + (n_dp - 1) + (n_ch - 1))

    tail = pltpu.make_async_remote_copy(
        src_ref=x.at[:, pl.ds(block_len - 16, 16), :], dst_ref=ext.at[:, pl.ds(0, 16), :],
        send_sem=tail_sem.at[0], recv_sem=tail_sem.at[1],
        device_id={"context": lax.rem(ctx + 1, n_ctx)}, device_id_type=MESH)

    @pl.when(ctx + 1 < n_ctx)
    def _():
        tail.start()


    w_steps = n_ch // 2

    quarter = columns // 4

    level = z % 2
    half_of = (odd + level) % 2
    given = 2 * half_of + level
    from_mate = 2 * (1 - half_of) + level
    from_next = 2 * (1 - half_of) + 1 - level

    def ring_link(way, step, arriving, start, count, send, recv):
        by = (1, n_ch - 1)[way]
        source = lax.rem(y + (n_ch - by) * (step if arriving else step - 1), n_ch)
        if step == w_steps:
            count = count // 2
            start = start + way * count
        lanes = pl.ds(pl.multiple_of(start, 128), count)
        return source, pltpu.make_async_remote_copy(
            src_ref=wall.at[source, :, lanes], dst_ref=wall.at[source, :, lanes],
            send_sem=send.at[way, step - 1], recv_sem=recv.at[way, step - 1],
            device_id={"channel": lax.rem(y + by, n_ch)}, device_id_type=MESH)

    def w_link(way, step, arriving):
        return ring_link(way, step, arriving, half_of * 2 * quarter, 2 * quarter, w_send, w_recv)

    def e_link(way, step, arriving):
        return ring_link(way, step, arriving, from_next * quarter, quarter, e_send, e_recv)

    def quarter_copy(source, place, send, recv, to):
        lanes = pl.ds(pl.multiple_of(place * quarter, 128), quarter)
        return pltpu.make_async_remote_copy(
            src_ref=wall.at[source, :, lanes], dst_ref=wall.at[source, :, lanes],
            send_sem=send.at[source], recv_sem=recv.at[source], device_id=to, device_id_type=MESH)

    def m_copy(source, arriving):
        return quarter_copy(source, from_mate if arriving else given, m_send, m_recv, mate)

    def u_copy(source, arriving):
        return quarter_copy(
            source, from_next if arriving else given, u_send, u_recv, {"context": 2 * chip(-1) + c})

    def give(source):
        m_copy(source, False).start()

        @pl.when(z >= 1)
        def _():
            u_copy(source, False).start()

    def pass_on(step):
        if step < w_steps:
            for way in (0, 1):
                w_link(way, step, True)[1].wait_recv()
                w_link(way, step + 1, False)[1].start()

            @pl.when(z + 1 == chips)
            def _():
                for way in (0, 1):
                    e_link(way, step, True)[1].wait_recv()
                    e_link(way, step + 1, False)[1].start()

            for way in (0, 1):
                give(lax.rem(y + (n_ch - (1, n_ch - 1)[way]) * step, n_ch))

    loads[4].wait()
    for way in (0, 1):
        w_link(way, 1, False)[1].start()

    @pl.when(z + 1 == chips)
    def _():
        for way in (0, 1):
            e_link(way, 1, False)[1].start()

    for by in range(1, n_dp):
        tap_copy(by).start()

    each_halo(lambda copy: copy.start(), (0, 1))

    for distance in (1, 2):
        @pl.when(z < distance)
        def _():
            rbuf[distance] = jnp.zeros(rbuf.shape[1:], BF16)

    @pl.when(ctx > 0)
    def _():
        tail.wait_recv()

    @pl.when(ctx == 0)
    def _():
        ext[:, pl.ds(0, 16), :] = jnp.zeros((3, 16, ext.shape[2]), BF16)

    for stream in range(3):
        ext[stream, pl.ds(0, 16), :] = (ext[stream, pl.ds(0, 16), :].astype(F32) * own_goes_on).astype(BF16)
    make_product(0, 16)
    each_halo(lambda copy: copy.start(), (2,))
    make_gate(0, 16)
    q_copy = pltpu.make_async_remote_copy(
        src_ref=qsend.at[1 - c], dst_ref=qbuf.at[c], send_sem=q_sem.at[0], recv_sem=q_sem.at[1],
        device_id=sibling, device_id_type=MESH)
    q_copy.start()
    qbuf[c] = qsend[c]
    rbuf[0, c] = pbuf[c]

    pass_on(1)

    loads[1].wait()
    loads[2].wait()
    for by in range(1, n_dp):
        tap_copy(by).wait_recv()
    tile = block_len // 2

    def filter_rows(i, carry):
        rows = pl.ds(pl.multiple_of(i * tile, tile), tile)
        fspec[rows, :] = lax.dot_general(
            fbuf[rows, :], tbuf[...].reshape(n_dp * HALF, block_len), (((1,), (1,)), ((), ())), preferred_element_type=F32)
        return carry

    take_in((0,))
    lax.fori_loop(0, 4, filter_rows, 0)
    pass_on(2)
    take_in((1, 2))

    step_rows = min(64, block_len // 2)
    tiles = block_len // step_rows

    def places(i):
        at = pl.multiple_of(i * step_rows, step_rows)
        return pl.ds(at, step_rows), pl.ds(block_len + at, step_rows)

    def combine(i, carry):
        re, im = places(i)
        sign = (1 - 2 * (i // (tiles // 2))).astype(F32)
        for d in range(n_dp + 1):
            real = imag = None
            if d > 0:
                lanes = pl.ds((d - 1) * HALF, HALF)
                real, imag = fspec[re, lanes], fspec[im, lanes]
            if d < n_dp:
                lanes = pl.ds(d * HALF, HALF)
                more_real, more_imag = sign * fspec[im, lanes], -sign * fspec[re, lanes]
                real = more_real if real is None else real + more_real
                imag = more_imag if imag is None else imag + more_imag
            gspec[d, re, :] = real
            gspec[d, im, :] = imag
        return carry

    lax.fori_loop(0, tiles, combine, 0)

    def transform(distance, keep_lo, keep_hi):
        lo, hi = rbuf[distance, 0], rbuf[distance, 1]
        if keep_lo is not None:
            lo = (lo.astype(F32) * keep_lo).astype(BF16)
            hi = (hi.astype(F32) * keep_hi).astype(BF16)
        both[:, :HALF] = lo
        both[:, HALF:] = hi

        def rows_of(i, carry):
            rows = pl.ds(pl.multiple_of(i * tile, tile), tile)
            spec[distance, rows, :] = jnp.dot(fbuf[rows, :], both[...], preferred_element_type=F32)
            return carry

        lax.fori_loop(0, 4, rows_of, 0)

    def term(d, distance, core, re, im):
        lanes = pl.ds(core * HALF, HALF)
        a, b = gspec[d, re, :], gspec[d, im, :]
        u, v = spec[distance, re, lanes], spec[distance, im, lanes]
        return a * u - b * v, a * v + b * u

    def terms(which, re, im):
        got = [term(d, distance, core, re, im) for d, distance, core in which]
        return sum(g[0] for g in got[1:]) + got[0][0], sum(g[1] for g in got[1:]) + got[0][1]

    for part in (0, 1, 2):
        halo_arrived(0, 1 - c, part)
    transform(0, None, None)
    transform(1, keep2, keep1)

    def early(i, carry):
        re, im = places(i)
        real, imag = terms([(0, 0, 0), (1, 1, 1), (2, 1, 0)], re, im)
        acc[0, re, :] = real
        acc[0, im, :] = imag
        real, imag = terms([(1, 0, 0), (2, 1, 1), (3, 1, 0)], re, im)
        acc[1, re, :] = real
        acc[1, im, :] = imag
        return carry

    lax.fori_loop(0, tiles, early, 0)
    pass_on(3)

    @pl.when(z >= 2)
    def _():
        for part in (0, 1, 2):
            for core in (0, 1):
                halo_arrived(2, core, part)

    transform(2, keep4, keep3)

    def late(i, carry):
        re, im = places(i)
        real, imag = terms([(3, 2, 1), (4, 2, 0)], re, im)
        total[re, pl.ds(0, HALF)] = (acc[0, re, :] + real).astype(BF16)
        total[im, pl.ds(0, HALF)] = (acc[0, im, :] + imag).astype(BF16)
        real, imag = terms([(4, 2, 1)], re, im)
        own_real, own_imag = terms([(0, 0, 1)], re, im)
        total[re, pl.ds(HALF, HALF)] = (own_real + keep_b * (acc[1, re, :] + real)).astype(BF16)
        total[im, pl.ds(HALF, HALF)] = (own_imag + keep_b * (acc[1, im, :] + imag)).astype(BF16)
        return carry

    lax.fori_loop(0, tiles, late, 0)

    loads[3].wait()
    pltpu.make_async_remote_copy(
        src_ref=qsend.at[1 - c], dst_ref=qbuf.at[1 - c], send_sem=q_sem.at[0], recv_sem=q_sem.at[1],
        device_id=sibling, device_id_type=MESH).wait_recv()
    pairs = n_ch // 2
    own_pair = y // 2
    other = y + 1 - 2 * (y % 2)

    def g_copy(to):
        return pltpu.make_async_remote_copy(
            src_ref=gown.at[to], dst_ref=gall.at[y], send_sem=g_send.at[to], recv_sem=g_recv.at[y],
            device_id={"channel": to}, device_id_type=MESH)

    def g_arrived(source):
        pltpu.make_async_remote_copy(
            src_ref=gown.at[source], dst_ref=gall.at[source], send_sem=g_send.at[source], recv_sem=g_recv.at[source],
            device_id={"channel": other}, device_id_type=MESH).wait_recv()

    def f_copy(source):
        return pltpu.make_async_remote_copy(
            src_ref=gall.at[source], dst_ref=gpair.at[source], send_sem=f_send.at[source], recv_sem=f_recv.at[source],
            device_id=partner, device_id_type=MESH)

    for k in range(pairs):
        pair = lax.rem(own_pair + k, pairs)
        rows = pl.ds(pl.multiple_of(pair * 2 * piece, 2 * piece), 2 * piece)
        conv = jnp.dot(ibuf[rows, :], total[...], preferred_element_type=F32)
        for block in (0, 1):
            got = (qbuf[block, rows, :].astype(F32) * conv[:, block * HALF:(block + 1) * HALF]).astype(BF16)
            for i in (0, 1):
                gown[2 * pair + i, pl.ds(block * piece, piece), :] = got[i * piece:(i + 1) * piece]
        if k == 0:
            g_copy(other).start()
            gall[y] = gown[y]
            f_copy(y).start()
        else:
            for i in (0, 1):
                g_copy(2 * pair + i).start()

    for way in (0, 1):
        w_link(way, w_steps, True)[1].wait_recv()
    give(lax.rem(y + w_steps, n_ch))

    def pieces(k):
        pair = lax.rem(own_pair - k + pairs, pairs)
        return 2 * pair, 2 * pair + 1

    def hand_on(k):
        for source in (other,) if k == 0 else pieces(k):
            g_arrived(source)
            f_copy(source).start()

    def tokens(k):
        first, second = pieces(k)
        own = jnp.concatenate([gall[first], gall[second]], 1)
        for source in (first, second):
            f_copy(source).wait_recv()
        return jnp.concatenate([own, jnp.concatenate([gpair[first], gpair[second]], 1)], 0)

    def weights(k, lanes):
        first, second = pieces(k)
        return jnp.concatenate([wall[first, :, lanes], wall[second, :, lanes]], 0)

    def project(k):
        part = jnp.dot(tokens(k), weights(k, slice(None)), preferred_element_type=F32)
        if k == 0:
            osum[...] = part
        else:
            osum[...] += part

    hand_on(0)
    hand_on(1)
    hand_on(2)
    for by in range(1, n_ch):
        m_copy(lax.rem(y + by, n_ch), True).wait_recv()

    @pl.when(z + 1 < chips)
    def _():
        for by in range(1, n_ch):
            u_copy(lax.rem(y + by, n_ch), True).wait_recv()

    @pl.when(z + 1 == chips)
    def _():
        for way in (0, 1):
            e_link(way, w_steps, True)[1].wait_recv()

    for k in range(pairs - 1):
        project(k)
        if k + 3 < pairs:
            hand_on(k + 3)

    mine = 2 * piece
    part_columns = columns // 2

    def p_copy(whose, h):
        return pltpu.make_async_remote_copy(
            src_ref=psend.at[whose, h], dst_ref=precv.at[whose, h],
            send_sem=p_send.at[whose, h], recv_sem=p_recv.at[whose, h],
            device_id=sibling, device_id_type=MESH)

    def back_copy(h):
        return pltpu.make_async_remote_copy(
            src_ref=rsend.at[h], dst_ref=rrecv.at[h], send_sem=r_send.at[h], recv_sem=r_recv.at[h],
            device_id=partner, device_id_type=MESH)

    def rows_of_block(whose, block):
        return pl.ds(pl.multiple_of(whose * mine + block * piece, piece), piece)

    last = tokens(pairs - 1)
    for h in (0, 1):
        lanes = pl.ds(h * part_columns, part_columns)
        osum[:, lanes] += jnp.dot(last, weights(pairs - 1, lanes), preferred_element_type=F32)
        for whose in (1, 0):
            psend[whose, h] = osum[rows_of_block(whose, 1 - c), lanes].astype(BF16)
            p_copy(whose, h).start()

    def whole(whose, h):
        p_copy(whose, h).wait_recv()
        lanes = pl.ds(h * part_columns, part_columns)
        return (osum[rows_of_block(whose, c), lanes] + precv[whose, h].astype(F32)).astype(BF16)

    def out_lanes(which, h):
        return pl.ds(pl.multiple_of(which * columns + h * part_columns, 128), part_columns)

    for h in (0, 1):
        rsend[h] = whole(1, h)
        back_copy(h).start()
    for h in (0, 1):
        out[:, out_lanes(side, h)] = whole(0, h)
    for h in (0, 1):
        back_copy(h).wait_recv()
        out[:, out_lanes(1 - side, h)] = rrecv[h]

    for h in (0, 1):
        back_copy(h).wait_send()
    q_copy.wait_send()
    for whose in (1, 0):
        for h in (0, 1):
            p_copy(whose, h).wait_send()
    for step in range(1, w_steps + 1):
        for way in (0, 1):
            w_link(way, step, False)[1].wait_send()
    f_copy(y).wait_send()

    @pl.when(z >= 1)
    def _():
        for by in range(1, n_ch):
            u_copy(lax.rem(y + by, n_ch), False).wait_send()

    @pl.when(z + 1 == chips)
    def _():
        for step in range(1, w_steps + 1):
            for way in (0, 1):
                e_link(way, step, False)[1].wait_send()

    for by in range(1, n_ch):
        g_copy(lax.rem(y + by, n_ch)).wait_send()
        m_copy(lax.rem(y + by, n_ch), False).wait_send()
        f_copy(lax.rem(y + by, n_ch)).wait_send()
    @pl.when(ctx + 1 < n_ctx)
    def _():
        tail.wait_send()

    for by in range(1, n_dp):
        tap_copy(by).wait_send()
    each_halo(lambda copy: copy.wait_send(), (0, 1, 2))

    @pl.when((z >= 1) & (z + 1 < chips))
    def _():
        for part in (0, 1, 2):
            for core in (0, 1):
                forward_copy(core, part).wait_send()


def per_device(mesh_shape, features, doc_start, short_taps, long_filter, w_out):
    block_len, channels, d_out = features.shape[1], features.shape[3], w_out.shape[1]
    n_ctx, n_ch, n_dp = mesh_shape["context"], mesh_shape["channel"], mesh_shape["dp"]
    streams = jnp.transpose(features[0], (1, 0, 2))
    forward, inverse = tables(block_len)
    piece, columns = block_len // n_ch, d_out // 2
    width = 2 * block_len
    anywhere = pl.BlockSpec(memory_space=pltpu.HBM)
    vmem = pl.BlockSpec(memory_space=pltpu.VMEM)
    dma = pltpu.SemaphoreType.DMA
    result = pl.pallas_call(
        functools.partial(kernel, (n_ctx, n_ch, n_dp, block_len, d_out)),
        out_shape=jax.ShapeDtypeStruct((piece, d_out), BF16),
        in_specs=[anywhere] * 7,
        out_specs=vmem,
        scratch_shapes=[
            pltpu.SMEM(doc_start.shape, jnp.int32),
            pltpu.VMEM(short_taps.shape, F32),
            pltpu.VMEM((3, 16 + block_len, channels), BF16),
            pltpu.VMEM((width, block_len), BF16),
            pltpu.VMEM((block_len, width), BF16),
            pltpu.VMEM((n_ch, HALF, columns), BF16),
            pltpu.VMEM((2, block_len, HALF), BF16),
            pltpu.VMEM((3, 2, block_len, HALF), BF16),
            pltpu.VMEM((n_dp, HALF, block_len), BF16),
            pltpu.VMEM((block_len, 2 * HALF), BF16),
            pltpu.VMEM((width, n_dp * HALF), F32),
            pltpu.VMEM((n_dp + 1, width, HALF), F32),
            pltpu.VMEM((3, width, 2 * HALF), F32),
            pltpu.VMEM((2, block_len, HALF), BF16),
            pltpu.VMEM((2, block_len, HALF), BF16),
            pltpu.VMEM((2, width, HALF), F32),
            pltpu.VMEM((width, 2 * HALF), BF16),
            pltpu.VMEM((n_ch, 2 * piece, HALF), BF16),
            pltpu.VMEM((n_ch, 2 * piece, HALF), BF16),
            pltpu.VMEM((n_ch, 2 * piece, HALF), BF16),
            pltpu.VMEM((4 * piece, columns), F32),
            pltpu.VMEM((2, 2, piece, columns // 2), BF16),
            pltpu.VMEM((2, 2, piece, columns // 2), BF16),
            pltpu.VMEM((2, piece, columns // 2), BF16),
            pltpu.VMEM((2, piece, columns // 2), BF16),
            dma((7,)), dma((2,)), dma((n_dp - 1,)), dma((n_dp - 1,)), dma((3, 2, 3)), dma((3, 2, 3)), dma((2,)),
            dma((2, n_ch // 2)), dma((2, n_ch // 2)), dma((2, n_ch // 2)), dma((2, n_ch // 2)),
            dma((n_ch,)), dma((n_ch,)), dma((n_ch,)), dma((n_ch,)), dma((n_ch,)), dma((n_ch,)), dma((n_ch,)), dma((n_ch,)),
            dma((2, 2)), dma((2, 2)), dma((2,)), dma((2,)),
        ],
        compiler_params=pltpu.CompilerParams(
            collective_id=0, has_side_effects=True, vmem_limit_bytes=60 * 1024 * 1024),
    )(doc_start, short_taps, streams, long_filter, w_out, forward, inverse)
    return result[None]


def solution(mesh):
    return jax.shard_map(
        functools.partial(per_device, dict(mesh.shape)),
        mesh=mesh,
        in_specs=(
            P("dp", "context", None, "channel"),
            P("dp", None),
            P(None, None, "channel"),
            P("channel", "dp"),
            P("channel", None),
        ),
        out_specs=P("dp", ("context", "channel"), None),
        check_vma=False,
    )
```

```python
import functools

import jax
import jax.numpy as jnp
import numpy as np
from jax import lax
from jax.experimental import pallas as pl
from jax.experimental.pallas import tpu as pltpu
from jax.sharding import PartitionSpec as P

MESH = pl.DeviceIdType.MESH
F32 = jnp.float32
BF16 = jnp.bfloat16
HALF = 128


def tables(block_len):
    freq = np.concatenate([np.arange(0, block_len, 2), np.arange(1, block_len, 2)])
    angle = 2.0 * np.pi * ((2 * freq[:, None] + 1) * np.arange(block_len)[None, :] % (4 * block_len)) / (4 * block_len)
    sign = np.where(freq % 2 == 0, 1.0, -1.0)[:, None]
    forward = np.concatenate([np.cos(angle), -np.sin(angle)], 0)
    inverse = np.concatenate([-sign * np.sin(angle), -sign * np.cos(angle)], 0).T / block_len
    return forward.astype(jnp.bfloat16), inverse.astype(jnp.bfloat16)


def kernel(
    sizes, doc_in, taps_in, x, filt, w, fwd, inv, out,
    doc, taps, ext, fbuf, ibuf, wall, pbuf, rbuf, tbuf, both, fspec, gspec, spec, qbuf, qsend, acc, total,
    gown, gall, gpair, osum, psend, precv, rsend, rrecv,
    load_sem, tail_sem, tap_send, tap_recv, halo_send, halo_recv, q_sem, w_send, w_recv, e_send, e_recv, m_send, m_recv, u_send, u_recv,
    g_send, g_recv, f_send, f_recv, p_send, p_recv, r_send, r_recv,
):
    n_ctx, n_ch, n_dp, block_len, d_out = sizes
    chips = n_ctx // 2
    ctx = lax.axis_index("context")
    y = lax.axis_index("channel")
    xi = lax.axis_index("dp")
    z = ctx // 2
    c = ctx % 2
    piece = block_len // n_ch
    columns = d_out // 2
    sibling = {"context": 2 * z + 1 - c}
    odd = xi % 2
    side = ((xi + 1) // 2) % 2
    partner = {"dp": xi + 1 - 2 * odd}
    mate = {"dp": lax.rem(xi + 2 * odd - 1 + n_dp, n_dp)}

    def chip(distance):
        return lax.rem(z + distance + chips, chips)

    barrier = pltpu.get_barrier_semaphore()
    pl.semaphore_signal(barrier, inc=1, device_id=sibling, device_id_type=MESH)

    @pl.when(z >= 1)
    def _():
        for core in (0, 1):
            pl.semaphore_signal(barrier, inc=1, device_id={"context": 2 * chip(-1) + core}, device_id_type=MESH)

    @pl.when(z + 1 < chips)
    def _():
        pl.semaphore_signal(barrier, inc=1, device_id={"context": 2 * chip(1) + c}, device_id_type=MESH)

    for by in range(1, n_dp):
        pl.semaphore_signal(barrier, inc=1, device_id={"dp": lax.rem(xi + by, n_dp)}, device_id_type=MESH)
    for by in range(1, n_ch):
        pl.semaphore_signal(barrier, inc=1, device_id={"channel": lax.rem(y + by, n_ch)}, device_id_type=MESH)

    own_rows = pl.ds(pl.multiple_of(c * HALF, HALF), HALF)
    loads = [
        pltpu.make_async_copy(x, ext.at[:, pl.ds(16, block_len), :], load_sem.at[0]),
        pltpu.make_async_copy(filt.at[own_rows, :], tbuf.at[xi], load_sem.at[1]),
        pltpu.make_async_copy(fwd, fbuf, load_sem.at[2]),
        pltpu.make_async_copy(inv, ibuf, load_sem.at[3]),
        pltpu.make_async_copy(
            w.at[own_rows, pl.ds(pl.multiple_of(side * columns, 128), columns)], wall.at[y], load_sem.at[4]),
        pltpu.make_async_copy(doc_in, doc, load_sem.at[5]),
        pltpu.make_async_copy(taps_in, taps, load_sem.at[6]),
    ]
    for load in loads:
        load.start()
    def tap_copy(by):
        return pltpu.make_async_remote_copy(
            src_ref=filt.at[own_rows, :], dst_ref=tbuf.at[xi],
            send_sem=tap_send.at[by - 1], recv_sem=tap_recv.at[by - 1],
            device_id={"dp": lax.rem(xi + by, n_dp)}, device_id_type=MESH)

    loads[5].wait()
    loads[6].wait()

    def goes_on(block):
        at = jnp.maximum(block, 0)
        return jnp.where((block > 0) & (doc[0, at] != 1), 1.0, 0.0).astype(F32)

    own_goes_on = goes_on(ctx)
    keep_b = goes_on(2 * z + 1)
    keep1 = goes_on(2 * z)
    keep2 = keep1 * goes_on(2 * z - 1)
    keep3 = keep2 * goes_on(2 * z - 2)
    keep4 = keep3 * goes_on(2 * z - 3)

    chunk = min(128, block_len)

    def smooth(stream, start, count):
        rows = ext[stream, pl.ds(start, count + 16), :].astype(F32)
        got = (
            taps[0, pl.ds(stream, 1), :] * rows
            + taps[1, pl.ds(stream, 1), :] * pltpu.roll(rows, 1, 0)
            + taps[2, pl.ds(stream, 1), :] * pltpu.roll(rows, 2, 0)
        )
        return got[16:]

    def make_product(start, count):
        product = (smooth(1, start, count) * smooth(2, start, count)).astype(BF16)
        pbuf[0, pl.ds(start, count), :] = product[:, :HALF]
        pbuf[1, pl.ds(start, count), :] = product[:, HALF:]

    def make_gate(start, count):
        smoothed = smooth(0, start, count).astype(BF16)
        qsend[0, pl.ds(start, count), :] = smoothed[:, :HALF]
        qsend[1, pl.ds(start, count), :] = smoothed[:, HALF:]

    middle = block_len // 2
    parts = (pl.ds(16, middle - 16), pl.ds(middle, middle), pl.ds(0, 16))

    def halo_copy(distance, half, part):
        return pltpu.make_async_remote_copy(
            src_ref=pbuf.at[half, parts[part], :], dst_ref=rbuf.at[distance, c, parts[part], :],
            send_sem=halo_send.at[distance, half, part], recv_sem=halo_recv.at[distance, c, part],
            device_id={"context": 2 * chip(distance) + half}, device_id_type=MESH)

    def forward_copy(core, part):
        return pltpu.make_async_remote_copy(
            src_ref=rbuf.at[1, core, parts[part], :], dst_ref=rbuf.at[2, core, parts[part], :],
            send_sem=halo_send.at[2, core, part], recv_sem=halo_recv.at[2, core, part],
            device_id={"context": 2 * chip(1) + c}, device_id_type=MESH)

    def halo_arrived(distance, core, part):
        pltpu.make_async_remote_copy(
            src_ref=pbuf.at[0, parts[part], :], dst_ref=rbuf.at[distance, core, parts[part], :],
            send_sem=halo_send.at[distance, 0, part], recv_sem=halo_recv.at[distance, core, part],
            device_id=sibling, device_id_type=MESH).wait_recv()

    def each_halo(act, parts_of):
        @pl.when(z + 1 < chips)
        def _():
            for part in parts_of:
                for half in (0, 1):
                    act(halo_copy(1, half, part))

        for part in parts_of:
            act(halo_copy(0, 1 - c, part))

    def take_in(parts_of):
        @pl.when(z >= 1)
        def _():
            for part in parts_of:
                for core in (0, 1):
                    halo_arrived(1, core, part)

        @pl.when((z >= 1) & (z + 1 < chips))
        def _():
            for part in parts_of:
                for core in (0, 1):
                    forward_copy(core, part).start()

    def make_products(lo, hi):
        for start in range(lo, hi, chunk):
            first = max(start, 16)
            make_product(first, start + chunk - first)

    loads[0].wait()
    make_products(0, block_len)
    for start in range(0, block_len, chunk):
        first = max(start, 16)
        make_gate(first, start + chunk - first)
    ahead = jnp.where(z + 1 < chips, 2, 0) + jnp.where(z >= 1, 1, 0)
    pl.semaphore_wait(barrier, 1 + ahead + (n_dp - 1) + (n_ch - 1))

    tail = pltpu.make_async_remote_copy(
        src_ref=x.at[:, pl.ds(block_len - 16, 16), :], dst_ref=ext.at[:, pl.ds(0, 16), :],
        send_sem=tail_sem.at[0], recv_sem=tail_sem.at[1],
        device_id={"context": lax.rem(ctx + 1, n_ctx)}, device_id_type=MESH)

    @pl.when(ctx + 1 < n_ctx)
    def _():
        tail.start()


    w_steps = n_ch // 2

    quarter = columns // 4

    level = z % 2
    half_of = (odd + level) % 2
    given = 2 * half_of + level
    from_mate = 2 * (1 - half_of) + level
    from_next = 2 * (1 - half_of) + 1 - level

    def ring_link(way, step, arriving, start, count, send, recv):
        by = (1, n_ch - 1)[way]
        source = lax.rem(y + (n_ch - by) * (step if arriving else step - 1), n_ch)
        if step == w_steps:
            count = count // 2
            start = start + way * count
        lanes = pl.ds(pl.multiple_of(start, 128), count)
        return source, pltpu.make_async_remote_copy(
            src_ref=wall.at[source, :, lanes], dst_ref=wall.at[source, :, lanes],
            send_sem=send.at[way, step - 1], recv_sem=recv.at[way, step - 1],
            device_id={"channel": lax.rem(y + by, n_ch)}, device_id_type=MESH)

    def w_link(way, step, arriving):
        return ring_link(way, step, arriving, half_of * 2 * quarter, 2 * quarter, w_send, w_recv)

    def e_link(way, step, arriving):
        return ring_link(way, step, arriving, from_next * quarter, quarter, e_send, e_recv)

    def quarter_copy(source, place, send, recv, to):
        lanes = pl.ds(pl.multiple_of(place * quarter, 128), quarter)
        return pltpu.make_async_remote_copy(
            src_ref=wall.at[source, :, lanes], dst_ref=wall.at[source, :, lanes],
            send_sem=send.at[source], recv_sem=recv.at[source], device_id=to, device_id_type=MESH)

    def m_copy(source, arriving):
        return quarter_copy(source, from_mate if arriving else given, m_send, m_recv, mate)

    def u_copy(source, arriving):
        return quarter_copy(
            source, from_next if arriving else given, u_send, u_recv, {"context": 2 * chip(-1) + c})

    def give(source):
        m_copy(source, False).start()

        @pl.when(z >= 1)
        def _():
            u_copy(source, False).start()

    def pass_on(step):
        if step < w_steps:
            for way in (0, 1):
                w_link(way, step, True)[1].wait_recv()
                w_link(way, step + 1, False)[1].start()

            @pl.when(z + 1 == chips)
            def _():
                for way in (0, 1):
                    e_link(way, step, True)[1].wait_recv()
                    e_link(way, step + 1, False)[1].start()

            for way in (0, 1):
                give(lax.rem(y + (n_ch - (1, n_ch - 1)[way]) * step, n_ch))

    loads[4].wait()
    for way in (0, 1):
        w_link(way, 1, False)[1].start()

    @pl.when(z + 1 == chips)
    def _():
        for way in (0, 1):
            e_link(way, 1, False)[1].start()

    for by in range(1, n_dp):
        tap_copy(by).start()

    each_halo(lambda copy: copy.start(), (0, 1))

    for distance in (1, 2):
        @pl.when(z < distance)
        def _():
            rbuf[distance] = jnp.zeros(rbuf.shape[1:], BF16)

    @pl.when(ctx > 0)
    def _():
        tail.wait_recv()

    @pl.when(ctx == 0)
    def _():
        ext[:, pl.ds(0, 16), :] = jnp.zeros((3, 16, ext.shape[2]), BF16)

    for stream in range(3):
        ext[stream, pl.ds(0, 16), :] = (ext[stream, pl.ds(0, 16), :].astype(F32) * own_goes_on).astype(BF16)
    make_product(0, 16)
    each_halo(lambda copy: copy.start(), (2,))
    make_gate(0, 16)
    q_copy = pltpu.make_async_remote_copy(
        src_ref=qsend.at[1 - c], dst_ref=qbuf.at[c], send_sem=q_sem.at[0], recv_sem=q_sem.at[1],
        device_id=sibling, device_id_type=MESH)
    q_copy.start()
    qbuf[c] = qsend[c]
    rbuf[0, c] = pbuf[c]

    pass_on(1)

    loads[1].wait()
    loads[2].wait()
    for by in range(1, n_dp):
        tap_copy(by).wait_recv()
    tile = block_len // 2

    def filter_rows(i, carry):
        rows = pl.ds(pl.multiple_of(i * tile, tile), tile)
        fspec[rows, :] = lax.dot_general(
            fbuf[rows, :], tbuf[...].reshape(n_dp * HALF, block_len), (((1,), (1,)), ((), ())), preferred_element_type=F32)
        return carry

    take_in((0,))
    lax.fori_loop(0, 4, filter_rows, 0)
    pass_on(2)
    take_in((1, 2))

    step_rows = min(64, block_len // 2)
    tiles = block_len // step_rows

    def places(i):
        at = pl.multiple_of(i * step_rows, step_rows)
        return pl.ds(at, step_rows), pl.ds(block_len + at, step_rows)

    def combine(i, carry):
        re, im = places(i)
        sign = (1 - 2 * (i // (tiles // 2))).astype(F32)
        for d in range(n_dp + 1):
            real = imag = None
            if d > 0:
                lanes = pl.ds((d - 1) * HALF, HALF)
                real, imag = fspec[re, lanes], fspec[im, lanes]
            if d < n_dp:
                lanes = pl.ds(d * HALF, HALF)
                more_real, more_imag = sign * fspec[im, lanes], -sign * fspec[re, lanes]
                real = more_real if real is None else real + more_real
                imag = more_imag if imag is None else imag + more_imag
            gspec[d, re, :] = real
            gspec[d, im, :] = imag
        return carry

    lax.fori_loop(0, tiles, combine, 0)

    def transform(distance, keep_lo, keep_hi):
        lo, hi = rbuf[distance, 0], rbuf[distance, 1]
        if keep_lo is not None:
            lo = (lo.astype(F32) * keep_lo).astype(BF16)
            hi = (hi.astype(F32) * keep_hi).astype(BF16)
        both[:, :HALF] = lo
        both[:, HALF:] = hi

        def rows_of(i, carry):
            rows = pl.ds(pl.multiple_of(i * tile, tile), tile)
            spec[distance, rows, :] = jnp.dot(fbuf[rows, :], both[...], preferred_element_type=F32)
            return carry

        lax.fori_loop(0, 4, rows_of, 0)

    def term(d, distance, core, re, im):
        lanes = pl.ds(core * HALF, HALF)
        a, b = gspec[d, re, :], gspec[d, im, :]
        u, v = spec[distance, re, lanes], spec[distance, im, lanes]
        return a * u - b * v, a * v + b * u

    def terms(which, re, im):
        got = [term(d, distance, core, re, im) for d, distance, core in which]
        return sum(g[0] for g in got[1:]) + got[0][0], sum(g[1] for g in got[1:]) + got[0][1]

    for part in (0, 1, 2):
        halo_arrived(0, 1 - c, part)
    transform(0, None, None)
    transform(1, keep2, keep1)

    def early(i, carry):
        re, im = places(i)
        real, imag = terms([(0, 0, 0), (1, 1, 1), (2, 1, 0)], re, im)
        acc[0, re, :] = real
        acc[0, im, :] = imag
        real, imag = terms([(1, 0, 0), (2, 1, 1), (3, 1, 0)], re, im)
        acc[1, re, :] = real
        acc[1, im, :] = imag
        return carry

    lax.fori_loop(0, tiles, early, 0)
    pass_on(3)

    @pl.when(z >= 2)
    def _():
        for part in (0, 1, 2):
            for core in (0, 1):
                halo_arrived(2, core, part)

    transform(2, keep4, keep3)

    def late(i, carry):
        re, im = places(i)
        real, imag = terms([(3, 2, 1), (4, 2, 0)], re, im)
        total[re, pl.ds(0, HALF)] = (acc[0, re, :] + real).astype(BF16)
        total[im, pl.ds(0, HALF)] = (acc[0, im, :] + imag).astype(BF16)
        real, imag = terms([(4, 2, 1)], re, im)
        own_real, own_imag = terms([(0, 0, 1)], re, im)
        total[re, pl.ds(HALF, HALF)] = (own_real + keep_b * (acc[1, re, :] + real)).astype(BF16)
        total[im, pl.ds(HALF, HALF)] = (own_imag + keep_b * (acc[1, im, :] + imag)).astype(BF16)
        return carry

    lax.fori_loop(0, tiles, late, 0)

    loads[3].wait()
    pltpu.make_async_remote_copy(
        src_ref=qsend.at[1 - c], dst_ref=qbuf.at[1 - c], send_sem=q_sem.at[0], recv_sem=q_sem.at[1],
        device_id=sibling, device_id_type=MESH).wait_recv()
    pairs = n_ch // 2
    own_pair = y // 2
    other = y + 1 - 2 * (y % 2)

    def g_copy(to):
        return pltpu.make_async_remote_copy(
            src_ref=gown.at[to], dst_ref=gall.at[y], send_sem=g_send.at[to], recv_sem=g_recv.at[y],
            device_id={"channel": to}, device_id_type=MESH)

    def g_arrived(source):
        pltpu.make_async_remote_copy(
            src_ref=gown.at[source], dst_ref=gall.at[source], send_sem=g_send.at[source], recv_sem=g_recv.at[source],
            device_id={"channel": other}, device_id_type=MESH).wait_recv()

    def f_copy(source):
        return pltpu.make_async_remote_copy(
            src_ref=gall.at[source], dst_ref=gpair.at[source], send_sem=f_send.at[source], recv_sem=f_recv.at[source],
            device_id=partner, device_id_type=MESH)

    for k in range(pairs):
        pair = lax.rem(own_pair + k, pairs)
        rows = pl.ds(pl.multiple_of(pair * 2 * piece, 2 * piece), 2 * piece)
        conv = jnp.dot(ibuf[rows, :], total[...], preferred_element_type=F32)
        for block in (0, 1):
            got = (qbuf[block, rows, :].astype(F32) * conv[:, block * HALF:(block + 1) * HALF]).astype(BF16)
            for i in (0, 1):
                gown[2 * pair + i, pl.ds(block * piece, piece), :] = got[i * piece:(i + 1) * piece]
        if k == 0:
            g_copy(other).start()
            gall[y] = gown[y]
            f_copy(y).start()
        else:
            for i in (0, 1):
                g_copy(2 * pair + i).start()

    for way in (0, 1):
        w_link(way, w_steps, True)[1].wait_recv()
    give(lax.rem(y + w_steps, n_ch))

    def pieces(k):
        pair = lax.rem(own_pair - k + pairs, pairs)
        return 2 * pair, 2 * pair + 1

    def hand_on(k):
        for source in (other,) if k == 0 else pieces(k):
            g_arrived(source)
            f_copy(source).start()

    def tokens(k):
        first, second = pieces(k)
        own = jnp.concatenate([gall[first], gall[second]], 1)
        for source in (first, second):
            f_copy(source).wait_recv()
        return jnp.concatenate([own, jnp.concatenate([gpair[first], gpair[second]], 1)], 0)

    def weights(k, lanes):
        first, second = pieces(k)
        return jnp.concatenate([wall[first, :, lanes], wall[second, :, lanes]], 0)

    def project(k):
        part = jnp.dot(tokens(k), weights(k, slice(None)), preferred_element_type=F32)
        if k == 0:
            osum[...] = part
        else:
            osum[...] += part

    hand_on(0)
    hand_on(1)
    hand_on(2)
    def weights_here(k):
        for source in (other,) if k == 0 else pieces(k):
            m_copy(source, True).wait_recv()

            @pl.when(z + 1 < chips)
            def _():
                u_copy(source, True).wait_recv()

        if k == pairs // 2:
            @pl.when(z + 1 == chips)
            def _():
                for way in (0, 1):
                    e_link(way, w_steps, True)[1].wait_recv()

    for k in range(pairs - 1):
        weights_here(k)
        project(k)
        if k + 3 < pairs:
            hand_on(k + 3)

    mine = 2 * piece
    part_columns = columns // 2

    def p_copy(whose, h):
        return pltpu.make_async_remote_copy(
            src_ref=psend.at[whose, h], dst_ref=precv.at[whose, h],
            send_sem=p_send.at[whose, h], recv_sem=p_recv.at[whose, h],
            device_id=sibling, device_id_type=MESH)

    def back_copy(h):
        return pltpu.make_async_remote_copy(
            src_ref=rsend.at[h], dst_ref=rrecv.at[h], send_sem=r_send.at[h], recv_sem=r_recv.at[h],
            device_id=partner, device_id_type=MESH)

    def rows_of_block(whose, block):
        return pl.ds(pl.multiple_of(whose * mine + block * piece, piece), piece)

    weights_here(pairs - 1)
    last = tokens(pairs - 1)
    for h in (0, 1):
        lanes = pl.ds(h * part_columns, part_columns)
        osum[:, lanes] += jnp.dot(last, weights(pairs - 1, lanes), preferred_element_type=F32)
        for whose in (1, 0):
            psend[whose, h] = osum[rows_of_block(whose, 1 - c), lanes].astype(BF16)
            p_copy(whose, h).start()

    def whole(whose, h):
        p_copy(whose, h).wait_recv()
        lanes = pl.ds(h * part_columns, part_columns)
        return (osum[rows_of_block(whose, c), lanes] + precv[whose, h].astype(F32)).astype(BF16)

    def out_lanes(which, h):
        return pl.ds(pl.multiple_of(which * columns + h * part_columns, 128), part_columns)

    for h in (0, 1):
        rsend[h] = whole(1, h)
        back_copy(h).start()
    for h in (0, 1):
        out[:, out_lanes(side, h)] = whole(0, h)
    for h in (0, 1):
        back_copy(h).wait_recv()
        out[:, out_lanes(1 - side, h)] = rrecv[h]

    for h in (0, 1):
        back_copy(h).wait_send()
    q_copy.wait_send()
    for whose in (1, 0):
        for h in (0, 1):
            p_copy(whose, h).wait_send()
    for step in range(1, w_steps + 1):
        for way in (0, 1):
            w_link(way, step, False)[1].wait_send()
    f_copy(y).wait_send()

    @pl.when(z >= 1)
    def _():
        for by in range(1, n_ch):
            u_copy(lax.rem(y + by, n_ch), False).wait_send()

    @pl.when(z + 1 == chips)
    def _():
        for step in range(1, w_steps + 1):
            for way in (0, 1):
                e_link(way, step, False)[1].wait_send()

    for by in range(1, n_ch):
        g_copy(lax.rem(y + by, n_ch)).wait_send()
        m_copy(lax.rem(y + by, n_ch), False).wait_send()
        f_copy(lax.rem(y + by, n_ch)).wait_send()
    @pl.when(ctx + 1 < n_ctx)
    def _():
        tail.wait_send()

    for by in range(1, n_dp):
        tap_copy(by).wait_send()
    each_halo(lambda copy: copy.wait_send(), (0, 1, 2))

    @pl.when((z >= 1) & (z + 1 < chips))
    def _():
        for part in (0, 1, 2):
            for core in (0, 1):
                forward_copy(core, part).wait_send()


def per_device(mesh_shape, features, doc_start, short_taps, long_filter, w_out):
    block_len, channels, d_out = features.shape[1], features.shape[3], w_out.shape[1]
    n_ctx, n_ch, n_dp = mesh_shape["context"], mesh_shape["channel"], mesh_shape["dp"]
    streams = jnp.transpose(features[0], (1, 0, 2))
    forward, inverse = tables(block_len)
    piece, columns = block_len // n_ch, d_out // 2
    width = 2 * block_len
    anywhere = pl.BlockSpec(memory_space=pltpu.HBM)
    vmem = pl.BlockSpec(memory_space=pltpu.VMEM)
    dma = pltpu.SemaphoreType.DMA
    result = pl.pallas_call(
        functools.partial(kernel, (n_ctx, n_ch, n_dp, block_len, d_out)),
        out_shape=jax.ShapeDtypeStruct((piece, d_out), BF16),
        in_specs=[anywhere] * 7,
        out_specs=vmem,
        scratch_shapes=[
            pltpu.SMEM(doc_start.shape, jnp.int32),
            pltpu.VMEM(short_taps.shape, F32),
            pltpu.VMEM((3, 16 + block_len, channels), BF16),
            pltpu.VMEM((width, block_len), BF16),
            pltpu.VMEM((block_len, width), BF16),
            pltpu.VMEM((n_ch, HALF, columns), BF16),
            pltpu.VMEM((2, block_len, HALF), BF16),
            pltpu.VMEM((3, 2, block_len, HALF), BF16),
            pltpu.VMEM((n_dp, HALF, block_len), BF16),
            pltpu.VMEM((block_len, 2 * HALF), BF16),
            pltpu.VMEM((width, n_dp * HALF), F32),
            pltpu.VMEM((n_dp + 1, width, HALF), F32),
            pltpu.VMEM((3, width, 2 * HALF), F32),
            pltpu.VMEM((2, block_len, HALF), BF16),
            pltpu.VMEM((2, block_len, HALF), BF16),
            pltpu.VMEM((2, width, HALF), F32),
            pltpu.VMEM((width, 2 * HALF), BF16),
            pltpu.VMEM((n_ch, 2 * piece, HALF), BF16),
            pltpu.VMEM((n_ch, 2 * piece, HALF), BF16),
            pltpu.VMEM((n_ch, 2 * piece, HALF), BF16),
            pltpu.VMEM((4 * piece, columns), F32),
            pltpu.VMEM((2, 2, piece, columns // 2), BF16),
            pltpu.VMEM((2, 2, piece, columns // 2), BF16),
            pltpu.VMEM((2, piece, columns // 2), BF16),
            pltpu.VMEM((2, piece, columns // 2), BF16),
            dma((7,)), dma((2,)), dma((n_dp - 1,)), dma((n_dp - 1,)), dma((3, 2, 3)), dma((3, 2, 3)), dma((2,)),
            dma((2, n_ch // 2)), dma((2, n_ch // 2)), dma((2, n_ch // 2)), dma((2, n_ch // 2)),
            dma((n_ch,)), dma((n_ch,)), dma((n_ch,)), dma((n_ch,)), dma((n_ch,)), dma((n_ch,)), dma((n_ch,)), dma((n_ch,)),
            dma((2, 2)), dma((2, 2)), dma((2,)), dma((2,)),
        ],
        compiler_params=pltpu.CompilerParams(
            collective_id=0, has_side_effects=True, vmem_limit_bytes=60 * 1024 * 1024),
    )(doc_start, short_taps, streams, long_filter, w_out, forward, inverse)
    return result[None]


def solution(mesh):
    return jax.shard_map(
        functools.partial(per_device, dict(mesh.shape)),
        mesh=mesh,
        in_specs=(
            P("dp", "context", None, "channel"),
            P("dp", None),
            P(None, None, "channel"),
            P("channel", "dp"),
            P("channel", None),
        ),
        out_specs=P("dp", ("context", "channel"), None),
        check_vma=False,
    )
```
